32 devices in a mesh: section: 2 (over x), seq: 4 (over z), chan: 4 (over y, core).
Axes of the slice: x: 2, y: 2, z: 4, core: 2. Of those that a mesh axis runs over, the one named last changes fastest.
Arguments:
- saved_input: bfloat16 [2, 2, 512, 1024], P('section', None, 'seq', 'chan'), may hold values from -6 to 6
- pre_gate: bfloat16 [2, 2, 512, 1024], P('section', None, 'seq', 'chan'), may hold values from -6 to 6
- post_gate: bfloat16 [2, 2, 512, 1024], P('section', None, 'seq', 'chan'), may hold values from -6 to 6
- grad_held: bfloat16 [2, 512, 1024], P('section', 'seq', 'chan'), may hold values from -6 to 6
- loss_grad: bfloat16 [512, 1024], P('seq', 'chan'), may hold values from -6 to 6
- filters: float32 [2, 512, 256], P('section', 'seq'), may hold values from -1 to 1
- skip_gain: float32 [2, 256], P('section'), may hold values from 0.5 to 1.5
Outputs:
- grad_out: bfloat16 [2, 512, 1024], P('section', 'seq', 'chan')
- filter_grad: float32 [2, 512, 256], P('section', 'seq', 'chan')
The draws below stay inside these ranges and needn't reach their ends.
All inputs are finite; a program needn't handle non-finite values.
Results may differ from the reference program's by a relative error of at most 0.017.
Values may be sent and summed in bfloat16 or wider, within the bound.
No kernel may reach another device: no remote copies, remote signals or barrier semaphores. Data moves between devices by JAX's collectives and lax.ppermute only.
A program may use at most 64 MiB of HBM per device.

```python
import math
import jax
import jax.numpy as jnp
from jax import lax

CH = 256
TICKS = 2
SECTIONS = 2
LEN = 512
WIDTH = 1024


def draw_filters(key, part):
    key_rate = jax.random.fold_in(key, 11)
    key_noise = jax.random.fold_in(key, 23)
    position = jnp.arange(LEN, dtype=jnp.float32)[None, :, None]
    decay_rate = jnp.exp(jax.random.uniform(key_rate, (SECTIONS, 1, CH), jnp.float32, math.log(0.3), math.log(LEN / 40.0)))
    noise_values = jnp.clip(jax.random.normal(key_noise, (SECTIONS, LEN, CH), jnp.float32), -4.0, 4.0)
    envelope = jnp.exp(-decay_rate * position / LEN)
    energy = -jnp.expm1(-2.0 * decay_rate) / -jnp.expm1(-2.0 * decay_rate / LEN)
    return noise_values * envelope / jnp.sqrt(energy)


def block_levels(stream_key, shape, pieces, smallest, high):
    def one(axis_at, blocks):
        draws = jax.random.uniform(jax.random.fold_in(jax.random.fold_in(stream_key, 6), axis_at), (blocks,), jnp.float32, smallest / len(pieces), high / len(pieces))
        return jnp.repeat(jnp.exp(draws), shape[axis_at] // blocks).reshape((-1,) + (1,) * (len(shape) - axis_at - 1))

    loudness = one(*pieces[0])
    for cut in pieces[1:]:
        loudness = loudness * one(*cut)
    return loudness


def bell_draw(key, dims, scale, most, shards=(), kind=jnp.bfloat16):
    gain = block_levels(key, dims, shards, -0.22, 0.18) if shards else 1.0
    entries = jax.random.normal(key, dims, jnp.float32) * scale * gain
    return jnp.minimum(jnp.maximum(entries, -most), most).astype(kind)


def setup_inputs(seed: int = 0) -> dict:
    seeds = jax.random.split(jax.random.key(seed), 8)
    saved_input = bell_draw(seeds[0], (SECTIONS, TICKS, LEN, WIDTH), 1.0, 6.0, ((0, 2), (2, 4), (3, 4)))
    pre_gate = bell_draw(seeds[1], (SECTIONS, TICKS, LEN, WIDTH), 1.0, 6.0, ((0, 2), (2, 4), (3, 4)))
    post_gate = bell_draw(seeds[2], (SECTIONS, TICKS, LEN, WIDTH), 1.0, 6.0, ((0, 2), (2, 4), (3, 4)))
    grad_held = bell_draw(seeds[3], (SECTIONS, LEN, WIDTH), 1.0, 6.0, ((0, 2), (1, 4), (2, 4)))
    loss_grad = bell_draw(seeds[4], (LEN, WIDTH), 1.0, 6.0, ((0, 4), (1, 4)))
    filters = draw_filters(jax.random.fold_in(seeds[7], 71), 0)
    skip_gain = jnp.clip(0.5 + 1.0 * jax.random.uniform(seeds[6], (SECTIONS, CH), jnp.float32) ** block_levels(seeds[6], (SECTIONS, CH), ((0, 2),), -0.2, 0.2), 0.5, 1.5)
    return dict(saved_input=saved_input, pre_gate=pre_gate, post_gate=post_gate, grad_held=grad_held, loss_grad=loss_grad, filters=filters, skip_gain=skip_gain)


def reference(saved_input, pre_gate, post_gate, grad_held, loss_grad, filters, skip_gain):
    section_count, tick_count, seq_length, width_all = saved_input.shape
    channel_count = filters.shape[2]
    slab_count = width_all // channel_count
    padded = 2 * seq_length
    kernel = jnp.tile(filters, (1, 1, slab_count))
    skip_full = jnp.tile(skip_gain, (1, slab_count))
    kernel_spec = jnp.fft.fft(kernel, n=padded, axis=1)
    carried = [grad_held[section_index].astype(jnp.float32) for section_index in range(section_count)]
    sums_list = [jnp.zeros((padded, width_all), dtype=kernel_spec.dtype) for section_index in range(section_count)]
    produced = []
    for tick_step in range(tick_count):
        produced = []
        new_sums = []
        for section_index in range(section_count):
            gate_in = pre_gate[section_index, tick_step].astype(jnp.float32)
            mixed_input = gate_in * saved_input[section_index, tick_step].astype(jnp.float32)
            gated_grad = post_gate[section_index, tick_step].astype(jnp.float32) * carried[section_index]
            gated_spec = jnp.fft.fft(gated_grad, n=padded, axis=0)
            mixed_spec = jnp.fft.fft(mixed_input, n=padded, axis=0)
            correlated = jnp.real(jnp.fft.ifft(jnp.conj(kernel_spec[section_index]) * gated_spec, axis=0))[:seq_length]
            gradient = (carried[section_index] + gate_in * (correlated + skip_full[section_index] * gated_grad)).astype(jnp.bfloat16)
            new_sums.append(sums_list[section_index] + gated_spec * jnp.conj(mixed_spec))
            produced.append(gradient)
        sums_list = new_sums
        if tick_step + 1 < tick_count:
            carried = [produced[section_index + 1].astype(jnp.float32) for section_index in range(section_count - 1)]
            carried = carried + [loss_grad.astype(jnp.float32)]
    grad_out = jnp.stack(produced)
    grad_scale = 1.0 / math.sqrt(seq_length * slab_count * tick_count)
    lag_list = []
    for section_index in range(section_count):
        lag_full = jnp.real(jnp.fft.ifft(sums_list[section_index], axis=0))[:seq_length]
        lag_list.append(lax.optimization_barrier(jnp.sum(lag_full.reshape(seq_length, slab_count, channel_count), axis=1)))
    filter_grad = (jnp.stack(lag_list) * grad_scale).astype(jnp.float32)
    return (grad_out, filter_grad)
```

```python
import functools
import math

import jax
import jax.numpy as jnp
import ml_dtypes
import numpy as np
from jax import lax
from jax.experimental import pallas as pl
from jax.experimental.pallas import tpu as pltpu
from jax.sharding import PartitionSpec as P

BF16 = jnp.bfloat16
F32 = jnp.float32
VMEM_LIMIT = 56 * 1024 * 1024


def transform_tables(length):
    odd = 2 * np.arange(length, dtype=np.int64) + 1
    angles = math.pi / (4 * length) * (odd[:, None] * odd[None, :] % (8 * length))
    table = np.concatenate([np.cos(angles), np.sin(angles)], axis=0)
    half_angle = math.pi / (4 * length) * odd
    turns = np.stack([np.cos(half_angle), np.sin(half_angle)])
    return table.astype(ml_dtypes.bfloat16), turns.astype(np.float32)


def call(kernel, out_shape, scratch=()):
    def run(index, *arrays):
        return pl.pallas_call(
            kernel,
            out_shape=out_shape,
            in_specs=[pl.BlockSpec(memory_space=pltpu.SMEM)]
            + [pl.BlockSpec(memory_space=pltpu.VMEM)] * len(arrays),
            scratch_shapes=scratch,
            compiler_params=pltpu.CompilerParams(vmem_limit_bytes=VMEM_LIMIT),
        )(index, *arrays)

    return run


def dot(left, right):
    return jnp.dot(left, right, preferred_element_type=F32)


def pack(arrays, stage, outs, seq_index):
    count = len(outs)
    unit = arrays[0].shape[1] // count
    for block in range(count):
        lanes = slice(block * unit, (block + 1) * unit)
        stage[block] = jnp.concatenate([array[:, lanes] for array in arrays], axis=1)
    for step, out in enumerate(outs):
        out[...] = stage[seq_index ^ step]


def pack_first(index, post, held, loss, pre, filters, *rest):
    outs, stage = rest[:-1], rest[-1]
    held_value = held[0]
    gated = (post[0, 0].astype(F32) * held_value.astype(F32)).astype(BF16)
    kept = jnp.where(index[1] == 0, loss[...], held_value)
    pack([gated, filters[0].astype(BF16), kept, pre[0, 0]], stage, outs, index[0])


def pack_second(index, saved, pre, post, *rest):
    outs, stage = rest[:-1], rest[-1]
    mixed = (saved[0].astype(F32) * pre[0].astype(F32)).astype(BF16)
    pack([mixed[0], mixed[1], post[0, 1], pre[0, 1]], stage, outs, index[0])


def gather_positions(chunks, held, seq_index):
    rows = chunks[0].shape[0]
    for step, chunk in enumerate(chunks):
        at = pl.multiple_of((seq_index ^ step) * rows, rows)
        held[pl.ds(at, rows), :] = chunk[...]


def turned(spectrum, turns):
    length = spectrum.shape[0] // 2
    real, imag = spectrum[:length], spectrum[length:]
    return real * turns[0] + imag * turns[1], imag * turns[0] - real * turns[1]


def times_conj(spectrum, other_real, other_imag):
    length = spectrum.shape[0] // 2
    real, imag = spectrum[:length], spectrum[length:]
    return real * other_real + imag * other_imag, imag * other_real - real * other_imag


def inverse(table, real, imag):
    length = table.shape[1]
    return dot(table[:length], real.astype(BF16)) + dot(table[length:], imag.astype(BF16))


def first_tick(index, gain, table, turns, *rest):
    chunks, (out, gated_spec, filter_spec, held) = rest[:-4], rest[-4:]
    length = held.shape[0]
    unit = held.shape[1] // 4
    gather_positions(chunks, held, index[0])
    spec = dot(table[...], held[:, : 2 * unit])
    spec, filters = spec[:, :unit], turned(spec[:, unit:], turns)
    gated_spec[...] = spec
    filter_spec[0], filter_spec[1] = filters
    correlated = inverse(table, *times_conj(spec, *filters)) * (1.0 / length)
    gated = held[:, :unit].astype(F32)
    kept = held[:, 2 * unit : 3 * unit]
    gate_in = held[:, 3 * unit :].astype(F32)
    gradient = (kept.astype(F32) + gate_in * (correlated + gain[...] * gated)).astype(BF16)
    gradient = jnp.where(index[1] == 0, kept, gradient)
    out[...] = jnp.concatenate([gradient[: length // 2], gradient[length // 2 :]], axis=1)


def mixed_spectra(index, table, turns, gated_spec, *rest):
    chunks, (gates, lag_spec, mixed_spec, held) = rest[:-4], rest[-4:]
    unit = held.shape[1] // 4
    gather_positions(chunks, held, index[0])
    gates[...] = held[:, 2 * unit :]
    spec = dot(table[...], held[:, : 2 * unit])
    first = turned(spec[:, :unit], turns)
    lag_spec[0], lag_spec[1] = times_conj(gated_spec[...], *first)
    mixed_spec[0], mixed_spec[1] = turned(spec[:, unit:], turns)


def second_tick(
    scale, index, gain, table, received, filter_spec, lag_spec, mixed_spec, gates, *rest
):
    outs, stage = rest[:-1], rest[-1]
    length = table.shape[1]
    unit = gain.shape[1]
    carried = jnp.concatenate([received[:, :unit], received[:, unit:]], axis=0).astype(F32)
    gated = (gates[:, :unit].astype(F32) * carried).astype(BF16)
    spec = dot(table[...], gated)
    filtered = times_conj(spec, filter_spec[0], filter_spec[1])
    lagged = times_conj(spec, mixed_spec[0], mixed_spec[1])
    real = jnp.concatenate([filtered[0], lag_spec[0] + lagged[0]], axis=1)
    imag = jnp.concatenate([filtered[1], lag_spec[1] + lagged[1]], axis=1)
    both = inverse(table, real, imag)
    correlated = both[:, :unit] * (1.0 / length)
    lag_grad = both[:, unit:] * (scale / length)
    gate_in = gates[:, unit:].astype(F32)
    gradient = carried + gate_in * (correlated + gain[...] * gated.astype(F32))
    result = jnp.concatenate([gradient, lag_grad], axis=1).astype(BF16)
    stage[...] = result.reshape(stage.shape)
    for step, out in enumerate(outs):
        out[...] = stage[index[0] ^ step]


def unpack(index, *rest):
    *refs, stage, lag_stage = rest
    count = stage.shape[0]
    chan_count = lag_stage.shape[0]
    chunks, grad, lags = refs[:count], refs[count], refs[count + 1 :]
    unit = stage.shape[2] // 2
    for step, chunk in enumerate(chunks):
        stage[index[0] ^ step] = chunk[...]
    grad[0] = jnp.concatenate([stage[block][:, :unit] for block in range(count)], axis=1)
    lag_grad = jnp.concatenate([stage[block][:, unit:] for block in range(count)], axis=1)
    lag_grad = lag_grad.astype(F32)
    width = lag_grad.shape[1] // chan_count
    for block in range(chan_count):
        lag_stage[block] = lag_grad[:, block * width : (block + 1) * width]
    for step, lag in enumerate(lags):
        lag[...] = lag_stage[index[2] ^ step]


def exchange(chunks, axis):
    size = lax.axis_size(axis)
    return [chunks[0]] + [
        lax.ppermute(chunks[step], axis, [(i, i ^ step) for i in range(size)])
        for step in range(1, size)
    ]


def body(table, turns, *args):
    saved_input, pre_gate, post_gate, grad_held, loss_grad, filters, skip_gain = args
    seq_count = lax.axis_size("seq")
    chan_count = lax.axis_size("chan")
    section_count = lax.axis_size("section")
    _, tick_count, rows, width = saved_input.shape
    length = rows * seq_count
    unit = width // seq_count
    seq_index = lax.axis_index("seq")
    index = jnp.stack([seq_index, lax.axis_index("section"), lax.axis_index("chan")])
    index = index.astype(jnp.int32)
    table = jnp.asarray(table)
    turns = jnp.asarray(np.broadcast_to(turns[:, :, None], (2, length, unit)))
    gain = lax.dynamic_slice(skip_gain, (0, seq_index * unit), (1, unit))
    struct = jax.ShapeDtypeStruct
    chunk = struct((rows, 4 * unit), BF16)
    stage = pltpu.VMEM((seq_count, rows, 4 * unit), BF16)
    held_rows = pltpu.VMEM((length, 4 * unit), BF16)
    spectrum = struct((2, length, unit), F32)

    first = call(pack_first, [chunk] * seq_count, [stage])(
        index, post_gate, grad_held, loss_grad, pre_gate, filters
    )
    first = exchange(first, "seq")
    second = call(pack_second, [chunk] * seq_count, [stage])(
        index, saved_input, pre_gate, post_gate
    )
    second = exchange(second, "seq")

    gradient, gated_spec, filter_spec = call(
        first_tick,
        [
            struct((length // 2, 2 * unit), BF16),
            struct((2 * length, unit), F32),
            spectrum,
        ],
        [held_rows],
    )(index, gain, table, turns, *first)
    ring = [(i, (i - 1) % section_count) for i in range(section_count)]
    received = lax.ppermute(gradient, "section", ring)

    gates, lag_spec, mixed_spec = call(
        mixed_spectra, [struct((length, 2 * unit), BF16), spectrum, spectrum], [held_rows]
    )(index, table, turns, gated_spec, *second)

    scale = 1.0 / math.sqrt(length * chan_count * tick_count)
    result = call(
        functools.partial(second_tick, scale),
        [struct((rows, 2 * unit), BF16)] * seq_count,
        [pltpu.VMEM((seq_count, rows, 2 * unit), BF16)],
    )(index, gain, table, received, filter_spec, lag_spec, mixed_spec, gates)
    result = exchange(result, "seq")

    lag_width = width // chan_count
    grad_out, *lags = call(
        unpack,
        [struct((1, rows, width), BF16)] + [struct((rows, lag_width), F32)] * chan_count,
        [
            pltpu.VMEM((seq_count, rows, 2 * unit), BF16),
            pltpu.VMEM((chan_count, rows, lag_width), F32),
        ],
    )(index, *result)
    lags = exchange(lags, "chan")
    return grad_out, functools.reduce(jnp.add, lags)[None]


def solution(mesh):
    placed = (
        P("section", None, "seq", "chan"),
        P("section", None, "seq", "chan"),
        P("section", None, "seq", "chan"),
        P("section", "seq", "chan"),
        P("seq", "chan"),
        P("section", "seq", None),
        P("section", None),
    )

    def program(*args):
        return jax.shard_map(
            functools.partial(body, *transform_tables(args[0].shape[2])),
            mesh=mesh,
            in_specs=placed,
            out_specs=(P("section", "seq", "chan"), P("section", "seq", "chan")),
            check_vma=False,
        )(*args)

    return program
```

```python
import functools
import math

import jax
import jax.numpy as jnp
import ml_dtypes
import numpy as np
from jax import lax
from jax.experimental import pallas as pl
from jax.experimental.pallas import tpu as pltpu
from jax.sharding import PartitionSpec as P

BF16 = jnp.bfloat16
F32 = jnp.float32


def transform_tables(length):
    odd = 2 * np.arange(length, dtype=np.int64) + 1
    angles = math.pi / (4 * length) * (odd[:, None] * odd[None, :] % (8 * length))
    table = np.concatenate([np.cos(angles), np.sin(angles)], axis=0)
    half_angle = math.pi / (4 * length) * odd
    turns = np.stack([np.cos(half_angle), np.sin(half_angle)])
    return table.astype(ml_dtypes.bfloat16), turns.astype(np.float32)


def size_of(shapes):
    total = 0
    for shape in shapes:
        lanes = -(-shape.shape[-1] // 128) * 128
        total += math.prod(shape.shape[:-1]) * lanes * jnp.dtype(shape.dtype).itemsize
    return total


def call(kernel, out_shape, scratch=()):
    def run(*arrays):
        held = size_of([*arrays, *out_shape, *scratch])
        return pl.pallas_call(
            kernel,
            out_shape=out_shape,
            in_specs=[pl.BlockSpec(memory_space=pltpu.VMEM)] * len(arrays),
            scratch_shapes=[pltpu.VMEM(shape.shape, shape.dtype) for shape in scratch],
            compiler_params=pltpu.CompilerParams(vmem_limit_bytes=2 * held + (4 << 20)),
        )(*arrays)

    return run


def dot(left, right):
    return jnp.dot(left, right, preferred_element_type=F32)


def pack(arrays, stage, outs):
    seq_index = lax.axis_index("seq")
    count = len(outs)
    unit = arrays[0].shape[1] // count
    for block in range(count):
        lanes = slice(block * unit, (block + 1) * unit)
        stage[block] = jnp.concatenate([array[:, lanes] for array in arrays], axis=1)
    for step, out in enumerate(outs):
        out[...] = stage[seq_index ^ step]


def pack_first(post, held, loss, pre, filters, *rest):
    outs, stage = rest[:-1], rest[-1]
    held_value = held[0]
    gated = (post[0, 0].astype(F32) * held_value.astype(F32)).astype(BF16)
    kept = jnp.where(lax.axis_index("section") == 0, loss[...], held_value)
    pack([gated, filters[0].astype(BF16), kept, pre[0, 0]], stage, outs)


def pack_second(after, saved, pre, post, *rest):
    del after
    outs, stage = rest[:-1], rest[-1]
    mixed = (saved[0].astype(F32) * pre[0].astype(F32)).astype(BF16)
    pack([mixed[0], mixed[1], post[0, 1], pre[0, 1]], stage, outs)


def gather_positions(chunks, held):
    seq_index = lax.axis_index("seq")
    rows = chunks[0].shape[0]
    for step, chunk in enumerate(chunks):
        at = pl.multiple_of((seq_index ^ step) * rows, rows)
        held[pl.ds(at, rows), :] = chunk[...]


def turned(spectrum, turns):
    length = spectrum.shape[0] // 2
    real, imag = spectrum[:length], spectrum[length:]
    return real * turns[0] + imag * turns[1], imag * turns[0] - real * turns[1]


def times_conj(spectrum, other_real, other_imag):
    length = spectrum.shape[0] // 2
    real, imag = spectrum[:length], spectrum[length:]
    return real * other_real + imag * other_imag, imag * other_real - real * other_imag


def inverse(table, real, imag):
    length = table.shape[1]
    return dot(table[:length], real.astype(BF16)) + dot(table[length:], imag.astype(BF16))


def first_tick(gain, table, turns, *rest):
    chunks, (out, gated_spec, filter_spec, held) = rest[:-4], rest[-4:]
    length = held.shape[0]
    unit = held.shape[1] // 4
    gather_positions(chunks, held)
    spec = dot(table[...], held[:, : 2 * unit])
    spec, filters = spec[:, :unit], turned(spec[:, unit:], turns)
    gated_spec[...] = spec
    filter_spec[0], filter_spec[1] = filters
    correlated = inverse(table, *times_conj(spec, *filters)) * (1.0 / length)
    gated = held[:, :unit].astype(F32)
    kept = held[:, 2 * unit : 3 * unit]
    gate_in = held[:, 3 * unit :].astype(F32)
    gradient = (kept.astype(F32) + gate_in * (correlated + gain[...] * gated)).astype(BF16)
    gradient = jnp.where(lax.axis_index("section") == 0, kept, gradient)
    out[...] = jnp.concatenate([gradient[: length // 2], gradient[length // 2 :]], axis=1)


def mixed_spectra(table, turns, gated_spec, *rest):
    chunks, (gates, lag_spec, mixed_spec, held) = rest[:-4], rest[-4:]
    unit = held.shape[1] // 4
    gather_positions(chunks, held)
    gates[...] = held[:, 2 * unit :]
    spec = dot(table[...], held[:, : 2 * unit])
    first = turned(spec[:, :unit], turns)
    lag_spec[0], lag_spec[1] = times_conj(gated_spec[...], *first)
    mixed_spec[0], mixed_spec[1] = turned(spec[:, unit:], turns)


def second_tick(
    scale, gain, table, received, filter_spec, lag_spec, mixed_spec, gates, *rest
):
    outs, stage = rest[:-1], rest[-1]
    length = table.shape[1]
    unit = gain.shape[1]
    carried = jnp.concatenate([received[:, :unit], received[:, unit:]], axis=0).astype(F32)
    gated = (gates[:, :unit].astype(F32) * carried).astype(BF16)
    spec = dot(table[...], gated)
    filtered = times_conj(spec, filter_spec[0], filter_spec[1])
    lagged = times_conj(spec, mixed_spec[0], mixed_spec[1])
    real = jnp.concatenate([filtered[0], lag_spec[0] + lagged[0]], axis=1)
    imag = jnp.concatenate([filtered[1], lag_spec[1] + lagged[1]], axis=1)
    both = inverse(table, real, imag)
    correlated = both[:, :unit] * (1.0 / length)
    lag_grad = both[:, unit:] * (scale / length)
    gate_in = gates[:, unit:].astype(F32)
    gradient = carried + gate_in * (correlated + gain[...] * gated.astype(F32))
    result = jnp.concatenate([gradient, lag_grad], axis=1).astype(BF16)
    stage[...] = result.reshape(stage.shape)
    for step, out in enumerate(outs):
        out[...] = stage[lax.axis_index("seq") ^ step]


def unpack(*rest):
    *refs, stage, lag_stage = rest
    count = stage.shape[0]
    chunks, grad, lags = refs[:count], refs[count], refs[count + 1 :]
    unit = stage.shape[2] // 2
    seq_index, chan_index = lax.axis_index("seq"), lax.axis_index("chan")
    for step, chunk in enumerate(chunks):
        stage[seq_index ^ step] = chunk[...]
    grad[0] = jnp.concatenate([stage[block][:, :unit] for block in range(count)], axis=1)
    lag_grad = jnp.concatenate([stage[block][:, unit:] for block in range(count)], axis=1)
    lag_stage[...] = lag_grad.astype(F32).T
    for step, lag in enumerate(lags):
        width = lag.shape[0]
        lag[...] = lag_stage[pl.ds(pl.multiple_of((chan_index ^ step) * width, width), width), :]


def add_up(*refs):
    *lags, out = refs
    out[...] = functools.reduce(jnp.add, [lag[...] for lag in lags])


def exchange(chunks, axis):
    size = lax.axis_size(axis)
    return [chunks[0]] + [
        lax.ppermute(chunks[step], axis, [(i, i ^ step) for i in range(size)])
        for step in range(1, size)
    ]


def body(table, turns, *args):
    saved_input, pre_gate, post_gate, grad_held, loss_grad, filters, skip_gain = args
    seq_count = lax.axis_size("seq")
    chan_count = lax.axis_size("chan")
    section_count = lax.axis_size("section")
    _, tick_count, rows, width = saved_input.shape
    length = rows * seq_count
    unit = width // seq_count
    seq_index = lax.axis_index("seq")
    table = jnp.asarray(table)
    turns = jnp.asarray(np.array(np.broadcast_to(turns[:, :, None], (2, length, unit))))
    gain = lax.dynamic_slice(skip_gain, (0, seq_index * unit), (1, unit))
    struct = jax.ShapeDtypeStruct
    chunk = struct((rows, 4 * unit), BF16)
    stage = struct((seq_count, rows, 4 * unit), BF16)
    held_rows = struct((length, 4 * unit), BF16)
    spectrum = struct((2, length, unit), F32)

    first = call(pack_first, [chunk] * seq_count, [stage])(
        post_gate, grad_held, loss_grad, pre_gate, filters
    )
    second = call(pack_second, [chunk] * seq_count, [stage])(
        first[0], saved_input, pre_gate, post_gate
    )
    first = exchange(first, "seq")
    second = exchange(second, "seq")

    gradient, gated_spec, filter_spec = call(
        first_tick,
        [
            struct((length // 2, 2 * unit), BF16),
            struct((2 * length, unit), F32),
            spectrum,
        ],
        [held_rows],
    )(gain, table, turns, *first)
    ring = [(i, (i - 1) % section_count) for i in range(section_count)]
    received = lax.ppermute(gradient, "section", ring)

    gates, lag_spec, mixed_spec = call(
        mixed_spectra, [struct((length, 2 * unit), BF16), spectrum, spectrum], [held_rows]
    )(table, turns, gated_spec, *second)

    scale = 1.0 / math.sqrt(length * chan_count * tick_count)
    result = call(
        functools.partial(second_tick, scale),
        [struct((rows, 2 * unit), BF16)] * seq_count,
        [struct((seq_count, rows, 2 * unit), BF16)],
    )(gain, table, received, filter_spec, lag_spec, mixed_spec, gates)
    result = exchange(result, "seq")

    lag_width = width // chan_count
    grad_out, *lags = call(
        unpack,
        [struct((1, rows, width), BF16)] + [struct((lag_width, rows), F32)] * chan_count,
        [
            struct((seq_count, rows, 2 * unit), BF16),
            struct((width, rows), F32),
        ],
    )(*result)
    lags = exchange(lags, "chan")
    (lag_grad,) = call(add_up, [struct((lag_width, rows), F32)])(*lags)
    return grad_out, lag_grad.T[None]


def solution(mesh):
    placed = (
        P("section", None, "seq", "chan"),
        P("section", None, "seq", "chan"),
        P("section", None, "seq", "chan"),
        P("section", "seq", "chan"),
        P("seq", "chan"),
        P("section", "seq", None),
        P("section", None),
    )

    def program(*args):
        return jax.shard_map(
            functools.partial(body, *transform_tables(args[0].shape[2])),
            mesh=mesh,
            in_specs=placed,
            out_specs=(P("section", "seq", "chan"), P("section", "seq", "chan")),
            check_vma=False,
        )(*args)

    return program
```

```python
import functools
import math

import jax
import jax.numpy as jnp
import ml_dtypes
import numpy as np
from jax import lax
from jax.experimental import pallas as pl
from jax.experimental.pallas import tpu as pltpu
from jax.sharding import PartitionSpec as P

BF16 = jnp.bfloat16
F32 = jnp.float32


def transform_tables(length):
    odd = 2 * np.arange(length, dtype=np.int64) + 1
    angles = math.pi / (4 * length) * (odd[:, None] * odd[None, :] % (8 * length))
    table = np.concatenate([np.cos(angles), np.sin(angles)], axis=0)
    half_angle = math.pi / (4 * length) * odd
    turns = np.stack([np.cos(half_angle), np.sin(half_angle)])
    return table.astype(ml_dtypes.bfloat16), turns.astype(np.float32)


def size_of(shapes):
    total = 0
    for shape in shapes:
        lanes = -(-shape.shape[-1] // 128) * 128
        total += math.prod(shape.shape[:-1]) * lanes * jnp.dtype(shape.dtype).itemsize
    return total


def call(kernel, out_shape, scratch=(), spaces=None, copies=0):
    def run(*arrays):
        held = size_of([*arrays, *out_shape, *scratch])
        if spaces:
            arrays = [
                pltpu.with_memory_space_constraint(array, space) if space == pltpu.HBM else array
                for array, space in zip(arrays, spaces)
            ]
        scratch_shapes = [pltpu.VMEM(shape.shape, shape.dtype) for shape in scratch]
        if copies:
            scratch_shapes.append(pltpu.SemaphoreType.DMA((copies,)))
        return pl.pallas_call(
            kernel,
            out_shape=out_shape,
            in_specs=[
                pl.BlockSpec(memory_space=space)
                for space in spaces or [pltpu.VMEM] * len(arrays)
            ],
            scratch_shapes=scratch_shapes,
            compiler_params=pltpu.CompilerParams(vmem_limit_bytes=2 * held + (4 << 20)),
        )(*arrays)

    return run


def fetch(sources, places, semaphores):
    copies = [
        pltpu.make_async_copy(source, place, semaphores.at[at])
        for at, (source, place) in enumerate(zip(sources, places))
    ]
    for copy in copies:
        copy.start()
    for copy in copies:
        copy.wait()


def dot(left, right):
    return jnp.dot(left, right, preferred_element_type=F32)


def pack(arrays, stage, outs):
    seq_index = lax.axis_index("seq")
    count = len(outs)
    unit = arrays[0].shape[1] // count
    for block in range(count):
        lanes = slice(block * unit, (block + 1) * unit)
        stage[block] = jnp.concatenate([array[:, lanes] for array in arrays], axis=1)
    for step, out in enumerate(outs):
        out[...] = stage[seq_index ^ step]


def pack_first(post, held, loss, pre, filters, *rest):
    *outs, stage, gates, lags, semaphores = rest
    sources = [post.at[0, 0], held.at[0], loss, pre.at[0, 0], filters.at[0]]
    fetch(sources, [gates.at[at] for at in range(4)] + [lags], semaphores)
    gated = (gates[0].astype(F32) * gates[1].astype(F32)).astype(BF16)
    kept = jnp.where(lax.axis_index("section") == 0, gates[2], gates[1])
    pack([gated, lags[...].astype(BF16), kept, gates[3]], stage, outs)


def pack_second(after, saved, pre, post, gains, table, turns, *rest):
    del after
    *outs, gain, table_out, turns_out, stage, gates, all_gains, semaphores = rest
    sources = [saved.at[0, 0], saved.at[0, 1], pre.at[0, 0], pre.at[0, 1], post.at[0, 1]]
    fetch(
        sources + [gains, table, turns],
        [gates.at[at] for at in range(5)] + [all_gains, table_out, turns_out],
        semaphores,
    )
    mixed = (gates[0:2].astype(F32) * gates[2:4].astype(F32)).astype(BF16)
    pack([mixed[0], mixed[1], gates[4], gates[3]], stage, outs)
    unit = gain.shape[1]
    for block in range(len(outs)):

        @pl.when(lax.axis_index("seq") == block)
        def _():
            gain[...] = all_gains[:, block * unit : (block + 1) * unit]


def gather_positions(chunks, held):
    seq_index = lax.axis_index("seq")
    rows = chunks[0].shape[0]
    for step, chunk in enumerate(chunks):
        at = pl.multiple_of((seq_index ^ step) * rows, rows)
        held[pl.ds(at, rows), :] = chunk[...]


def turned(spectrum, turns):
    length = spectrum.shape[0] // 2
    real, imag = spectrum[:length], spectrum[length:]
    return real * turns[0] + imag * turns[1], imag * turns[0] - real * turns[1]


def times_conj(spectrum, other_real, other_imag):
    length = spectrum.shape[0] // 2
    real, imag = spectrum[:length], spectrum[length:]
    return real * other_real + imag * other_imag, imag * other_real - real * other_imag


def inverse(table, real, imag):
    length = table.shape[1]
    return dot(table[:length], real.astype(BF16)) + dot(table[length:], imag.astype(BF16))


def first_tick(gain, table, turns, *rest):
    chunks, (out, gated_spec, filter_spec, held) = rest[:-4], rest[-4:]
    length = held.shape[0]
    unit = held.shape[1] // 4
    gather_positions(chunks, held)
    spec = dot(table[...], held[:, : 2 * unit])
    spec, filters = spec[:, :unit], turned(spec[:, unit:], turns)
    gated_spec[...] = spec
    filter_spec[0], filter_spec[1] = filters
    correlated = inverse(table, *times_conj(spec, *filters)) * (1.0 / length)
    gated = held[:, :unit].astype(F32)
    kept = held[:, 2 * unit : 3 * unit]
    gate_in = held[:, 3 * unit :].astype(F32)
    gradient = (kept.astype(F32) + gate_in * (correlated + gain[...] * gated)).astype(BF16)
    gradient = jnp.where(lax.axis_index("section") == 0, kept, gradient)
    out[...] = jnp.concatenate([gradient[: length // 2], gradient[length // 2 :]], axis=1)


def mixed_spectra(table, turns, gated_spec, *rest):
    chunks, (gates, lag_spec, mixed_spec, held) = rest[:-4], rest[-4:]
    unit = held.shape[1] // 4
    gather_positions(chunks, held)
    gates[...] = held[:, 2 * unit :]
    spec = dot(table[...], held[:, : 2 * unit])
    first = turned(spec[:, :unit], turns)
    lag_spec[0], lag_spec[1] = times_conj(gated_spec[...], *first)
    mixed_spec[0], mixed_spec[1] = turned(spec[:, unit:], turns)


def second_tick(
    scale, gain, table, received, filter_spec, lag_spec, mixed_spec, gates, *rest
):
    outs, stage = rest[:-1], rest[-1]
    length = table.shape[1]
    unit = gain.shape[1]
    carried = jnp.concatenate([received[:, :unit], received[:, unit:]], axis=0).astype(F32)
    gated = (gates[:, :unit].astype(F32) * carried).astype(BF16)
    spec = dot(table[...], gated)
    filtered = times_conj(spec, filter_spec[0], filter_spec[1])
    lagged = times_conj(spec, mixed_spec[0], mixed_spec[1])
    real = jnp.concatenate([filtered[0], lag_spec[0] + lagged[0]], axis=1)
    imag = jnp.concatenate([filtered[1], lag_spec[1] + lagged[1]], axis=1)
    both = inverse(table, real, imag)
    correlated = both[:, :unit] * (1.0 / length)
    lag_grad = both[:, unit:] * (scale / length)
    gate_in = gates[:, unit:].astype(F32)
    gradient = carried + gate_in * (correlated + gain[...] * gated.astype(F32))
    result = jnp.concatenate([gradient, lag_grad], axis=1).astype(BF16)
    stage[...] = result.reshape(stage.shape)
    for step, out in enumerate(outs):
        out[...] = stage[lax.axis_index("seq") ^ step]


def unpack(*rest):
    *refs, stage, lag_stage = rest
    count = stage.shape[0]
    chunks, grad, lags = refs[:count], refs[count], refs[count + 1 :]
    unit = stage.shape[2] // 2
    seq_index, chan_index = lax.axis_index("seq"), lax.axis_index("chan")
    for step, chunk in enumerate(chunks):
        stage[seq_index ^ step] = chunk[...]
    grad[0] = jnp.concatenate([stage[block][:, :unit] for block in range(count)], axis=1)
    lag_grad = jnp.concatenate([stage[block][:, unit:] for block in range(count)], axis=1)
    lag_stage[...] = lag_grad.astype(F32).T
    for step, lag in enumerate(lags):
        width = lag.shape[0]
        lag[...] = lag_stage[pl.ds(pl.multiple_of((chan_index ^ step) * width, width), width), :]


def add_up(*refs):
    *lags, out = refs
    out[...] = functools.reduce(jnp.add, [lag[...] for lag in lags])


def exchange(chunks, axis):
    size = lax.axis_size(axis)
    return [chunks[0]] + [
        lax.ppermute(chunks[step], axis, [(i, i ^ step) for i in range(size)])
        for step in range(1, size)
    ]


def body(table, turns, *args):
    saved_input, pre_gate, post_gate, grad_held, loss_grad, filters, skip_gain = args
    seq_count = lax.axis_size("seq")
    chan_count = lax.axis_size("chan")
    section_count = lax.axis_size("section")
    _, tick_count, rows, width = saved_input.shape
    length = rows * seq_count
    unit = width // seq_count
    table = jnp.asarray(table)
    turns = jnp.asarray(np.array(np.broadcast_to(turns[:, :, None], (2, length, unit))))
    struct = jax.ShapeDtypeStruct
    chunk = struct((rows, 4 * unit), BF16)
    stage = struct((seq_count, rows, 4 * unit), BF16)
    held_rows = struct((length, 4 * unit), BF16)
    spectrum = struct((2, length, unit), F32)

    first = call(
        pack_first,
        [chunk] * seq_count,
        [stage, struct((4, rows, width), BF16), struct((rows, width), F32)],
        [pltpu.HBM] * 5,
        5,
    )(post_gate, grad_held, loss_grad, pre_gate, filters)
    *second, gain, table, turns = call(
        pack_second,
        [chunk] * seq_count
        + [
            struct((1, unit), F32),
            struct(table.shape, BF16),
            struct(turns.shape, F32),
        ],
        [stage, struct((5, rows, width), BF16), struct((1, width), F32)],
        [pl.ANY] + [pltpu.HBM] * 6,
        8,
    )(first[0], saved_input, pre_gate, post_gate, skip_gain, table, turns)
    first = exchange(first, "seq")
    second = exchange(second, "seq")

    gradient, gated_spec, filter_spec = call(
        first_tick,
        [
            struct((length // 2, 2 * unit), BF16),
            struct((2 * length, unit), F32),
            spectrum,
        ],
        [held_rows],
    )(gain, table, turns, *first)
    ring = [(i, (i - 1) % section_count) for i in range(section_count)]
    received = lax.ppermute(gradient, "section", ring)

    gates, lag_spec, mixed_spec = call(
        mixed_spectra, [struct((length, 2 * unit), BF16), spectrum, spectrum], [held_rows]
    )(table, turns, gated_spec, *second)

    scale = 1.0 / math.sqrt(length * chan_count * tick_count)
    result = call(
        functools.partial(second_tick, scale),
        [struct((rows, 2 * unit), BF16)] * seq_count,
        [struct((seq_count, rows, 2 * unit), BF16)],
    )(gain, table, received, filter_spec, lag_spec, mixed_spec, gates)
    result = exchange(result, "seq")

    lag_width = width // chan_count
    grad_out, *lags = call(
        unpack,
        [struct((1, rows, width), BF16)] + [struct((lag_width, rows), F32)] * chan_count,
        [
            struct((seq_count, rows, 2 * unit), BF16),
            struct((width, rows), F32),
        ],
    )(*result)
    lags = exchange(lags, "chan")
    (lag_grad,) = call(add_up, [struct((lag_width, rows), F32)])(*lags)
    return grad_out, lag_grad.T[None]


def solution(mesh):
    placed = (
        P("section", None, "seq", "chan"),
        P("section", None, "seq", "chan"),
        P("section", None, "seq", "chan"),
        P("section", "seq", "chan"),
        P("seq", "chan"),
        P("section", "seq", None),
        P("section", None),
    )

    def program(*args):
        return jax.shard_map(
            functools.partial(body, *transform_tables(args[0].shape[2])),
            mesh=mesh,
            in_specs=placed,
            out_specs=(P("section", "seq", "chan"), P("section", "seq", "chan")),
            check_vma=False,
        )(*args)

    return program
```

```python
import functools
import math

import jax
import jax.numpy as jnp
import ml_dtypes
import numpy as np
from jax import lax
from jax.experimental import pallas as pl
from jax.experimental.pallas import tpu as pltpu
from jax.sharding import PartitionSpec as P

BF16 = jnp.bfloat16
F32 = jnp.float32


def transform_tables(length):
    odd = 2 * np.arange(length, dtype=np.int64) + 1
    angles = math.pi / (4 * length) * (odd[:, None] * odd[None, :] % (8 * length))
    table = np.concatenate([np.cos(angles), np.sin(angles)], axis=0)
    half_angle = math.pi / (4 * length) * odd
    turns = np.stack([np.cos(half_angle), np.sin(half_angle)])
    return table.astype(ml_dtypes.bfloat16), turns.astype(np.float32)


def size_of(shapes):
    total = 0
    for shape in shapes:
        lanes = -(-shape.shape[-1] // 128) * 128
        total += math.prod(shape.shape[:-1]) * lanes * jnp.dtype(shape.dtype).itemsize
    return total


def call(kernel, out_shape, scratch=(), spaces=None, copies=0):
    def run(*arrays):
        held = size_of([*arrays, *out_shape, *scratch])
        if spaces:
            arrays = [
                pltpu.with_memory_space_constraint(array, space) if space == pltpu.HBM else array
                for array, space in zip(arrays, spaces)
            ]
        scratch_shapes = [pltpu.VMEM(shape.shape, shape.dtype) for shape in scratch]
        if copies:
            scratch_shapes.append(pltpu.SemaphoreType.DMA((copies,)))
        return pl.pallas_call(
            kernel,
            out_shape=out_shape,
            in_specs=[
                pl.BlockSpec(memory_space=space)
                for space in spaces or [pltpu.VMEM] * len(arrays)
            ],
            scratch_shapes=scratch_shapes,
            compiler_params=pltpu.CompilerParams(vmem_limit_bytes=2 * held + (4 << 20)),
        )(*arrays)

    return run


def fetch(sources, places, semaphores):
    copies = [
        pltpu.make_async_copy(source, place, semaphores.at[at])
        for at, (source, place) in enumerate(zip(sources, places))
    ]
    for copy in copies:
        copy.start()
    for copy in copies:
        copy.wait()


def dot(left, right):
    return jnp.dot(left, right, preferred_element_type=F32)


def pack(arrays, stage, outs):
    seq_index = lax.axis_index("seq")
    count = len(outs)
    unit = arrays[0].shape[1] // count
    for block in range(count):
        lanes = slice(block * unit, (block + 1) * unit)
        stage[block] = jnp.concatenate([array[:, lanes] for array in arrays], axis=1)
    for step, out in enumerate(outs):
        out[...] = stage[seq_index ^ step]


def pack_first(post, held, loss, pre, filters, *rest):
    *outs, stage, gates, lags, semaphores = rest
    sources = [post.at[0, 0], held.at[0], loss, pre.at[0, 0], filters.at[0]]
    fetch(sources, [gates.at[at] for at in range(4)] + [lags], semaphores)
    gated = (gates[0].astype(F32) * gates[1].astype(F32)).astype(BF16)
    kept = jnp.where(lax.axis_index("section") == 0, gates[2], gates[1])
    pack([gated, lags[...].astype(BF16), kept, gates[3]], stage, outs)


def pack_second(after, saved, pre, post, gains, table, turns, *rest):
    del after
    *outs, gain, table_out, turns_out, stage, gates, all_gains, semaphores = rest
    sources = [saved.at[0, 0], saved.at[0, 1], pre.at[0, 0], pre.at[0, 1], post.at[0, 1]]
    fetch(
        sources + [gains, table, turns],
        [gates.at[at] for at in range(5)] + [all_gains, table_out, turns_out],
        semaphores,
    )
    mixed = (gates[0:2].astype(F32) * gates[2:4].astype(F32)).astype(BF16)
    pack([mixed[0], mixed[1], gates[4], gates[3]], stage, outs)
    unit = gain.shape[1]
    for block in range(len(outs)):

        @pl.when(lax.axis_index("seq") == block)
        def _():
            gain[...] = all_gains[:, block * unit : (block + 1) * unit]


def gather_positions(chunks, steps, held):
    seq_index = lax.axis_index("seq")
    rows = chunks[0].shape[0]
    for step, chunk in zip([0, *steps], chunks):
        at = pl.multiple_of((seq_index ^ step) * rows, rows)
        held[pl.ds(at, rows), :] = chunk[...]


def turned(spectrum, turns):
    length = spectrum.shape[0] // 2
    real, imag = spectrum[:length], spectrum[length:]
    return real * turns[0] + imag * turns[1], imag * turns[0] - real * turns[1]


def times_conj(spectrum, other_real, other_imag):
    length = spectrum.shape[0] // 2
    real, imag = spectrum[:length], spectrum[length:]
    return real * other_real + imag * other_imag, imag * other_real - real * other_imag


def inverse(table, real, imag):
    length = table.shape[1]
    return dot(table[:length], real.astype(BF16)) + dot(table[length:], imag.astype(BF16))


def first_tick(gain, table, turns, *rest):
    chunks, (out, gated_spec, filter_spec, held) = rest[:-4], rest[-4:]
    length = held.shape[0]
    unit = held.shape[1] // 4
    gather_positions(chunks, middle_first(len(chunks)), held)
    spec = dot(table[...], held[:, : 2 * unit])
    spec, filters = spec[:, :unit], turned(spec[:, unit:], turns)
    gated_spec[...] = spec
    filter_spec[0], filter_spec[1] = filters
    correlated = inverse(table, *times_conj(spec, *filters)) * (1.0 / length)
    gated = held[:, :unit].astype(F32)
    kept = held[:, 2 * unit : 3 * unit]
    gate_in = held[:, 3 * unit :].astype(F32)
    gradient = (kept.astype(F32) + gate_in * (correlated + gain[...] * gated)).astype(BF16)
    gradient = jnp.where(lax.axis_index("section") == 0, kept, gradient)
    out[...] = jnp.concatenate([gradient[: length // 2], gradient[length // 2 :]], axis=1)


def mixed_spectra(table, turns, gated_spec, *rest):
    chunks, (gates, lag_spec, mixed_spec, held) = rest[:-4], rest[-4:]
    unit = held.shape[1] // 4
    gather_positions(chunks, near_first(len(chunks)), held)
    gates[...] = held[:, 2 * unit :]
    spec = dot(table[...], held[:, : 2 * unit])
    first = turned(spec[:, :unit], turns)
    lag_spec[0], lag_spec[1] = times_conj(gated_spec[...], *first)
    mixed_spec[0], mixed_spec[1] = turned(spec[:, unit:], turns)


def second_tick(
    scale, gain, table, received, filter_spec, lag_spec, mixed_spec, gates, *rest
):
    outs, stage = rest[:-1], rest[-1]
    length = table.shape[1]
    unit = gain.shape[1]
    carried = jnp.concatenate([received[:, :unit], received[:, unit:]], axis=0).astype(F32)
    gated = (gates[:, :unit].astype(F32) * carried).astype(BF16)
    spec = dot(table[...], gated)
    filtered = times_conj(spec, filter_spec[0], filter_spec[1])
    lagged = times_conj(spec, mixed_spec[0], mixed_spec[1])
    real = jnp.concatenate([filtered[0], lag_spec[0] + lagged[0]], axis=1)
    imag = jnp.concatenate([filtered[1], lag_spec[1] + lagged[1]], axis=1)
    both = inverse(table, real, imag)
    correlated = both[:, :unit] * (1.0 / length)
    lag_grad = both[:, unit:] * (scale / length)
    gate_in = gates[:, unit:].astype(F32)
    gradient = carried + gate_in * (correlated + gain[...] * gated.astype(F32))
    result = jnp.concatenate([gradient, lag_grad], axis=1).astype(BF16)
    stage[...] = result.reshape(stage.shape)
    for step, out in enumerate(outs):
        out[...] = stage[lax.axis_index("seq") ^ step]


def unpack(*rest):
    *refs, stage, lag_stage = rest
    count = stage.shape[0]
    chunks, grad, lags = refs[:count], refs[count], refs[count + 1 :]
    unit = stage.shape[2] // 2
    seq_index, chan_index = lax.axis_index("seq"), lax.axis_index("chan")
    for step, chunk in zip([0, *middle_first(count)], chunks):
        stage[seq_index ^ step] = chunk[...]
    grad[0] = jnp.concatenate([stage[block][:, :unit] for block in range(count)], axis=1)
    lag_grad = jnp.concatenate([stage[block][:, unit:] for block in range(count)], axis=1)
    lag_stage[...] = lag_grad.astype(F32).T
    for step, lag in enumerate(lags):
        width = lag.shape[0]
        lag[...] = lag_stage[pl.ds(pl.multiple_of((chan_index ^ step) * width, width), width), :]


def add_up(*refs):
    *lags, out = refs
    out[...] = functools.reduce(jnp.add, [lag[...] for lag in lags])


def exchange(chunks, axis, steps):
    size = lax.axis_size(axis)
    return [chunks[0]] + [
        lax.ppermute(chunks[step], axis, [(i, i ^ step) for i in range(size)]) for step in steps
    ]


def middle_first(size):
    return [*range(2, size), 1]


def near_first(size):
    return list(range(1, size))


def far_first(size):
    return list(reversed(range(1, size)))


def body(table, turns, *args):
    saved_input, pre_gate, post_gate, grad_held, loss_grad, filters, skip_gain = args
    seq_count = lax.axis_size("seq")
    chan_count = lax.axis_size("chan")
    section_count = lax.axis_size("section")
    _, tick_count, rows, width = saved_input.shape
    length = rows * seq_count
    unit = width // seq_count
    table = jnp.asarray(table)
    turns = jnp.asarray(np.array(np.broadcast_to(turns[:, :, None], (2, length, unit))))
    struct = jax.ShapeDtypeStruct
    chunk = struct((rows, 4 * unit), BF16)
    stage = struct((seq_count, rows, 4 * unit), BF16)
    held_rows = struct((length, 4 * unit), BF16)
    spectrum = struct((2, length, unit), F32)

    first = call(
        pack_first,
        [chunk] * seq_count,
        [stage, struct((4, rows, width), BF16), struct((rows, width), F32)],
        [pltpu.HBM] * 5,
        5,
    )(post_gate, grad_held, loss_grad, pre_gate, filters)
    *second, gain, table, turns = call(
        pack_second,
        [chunk] * seq_count
        + [
            struct((1, unit), F32),
            struct(table.shape, BF16),
            struct(turns.shape, F32),
        ],
        [stage, struct((5, rows, width), BF16), struct((1, width), F32)],
        [pl.ANY] + [pltpu.HBM] * 6,
        8,
    )(first[0], saved_input, pre_gate, post_gate, skip_gain, table, turns)
    first = exchange(first, "seq", middle_first(seq_count))
    second = exchange(second, "seq", near_first(seq_count))

    gradient, gated_spec, filter_spec = call(
        first_tick,
        [
            struct((length // 2, 2 * unit), BF16),
            struct((2 * length, unit), F32),
            spectrum,
        ],
        [held_rows],
    )(gain, table, turns, *first)
    ring = [(i, (i - 1) % section_count) for i in range(section_count)]
    received = lax.ppermute(gradient, "section", ring)

    gates, lag_spec, mixed_spec = call(
        mixed_spectra, [struct((length, 2 * unit), BF16), spectrum, spectrum], [held_rows]
    )(table, turns, gated_spec, *second)

    scale = 1.0 / math.sqrt(length * chan_count * tick_count)
    result = call(
        functools.partial(second_tick, scale),
        [struct((rows, 2 * unit), BF16)] * seq_count,
        [struct((seq_count, rows, 2 * unit), BF16)],
    )(gain, table, received, filter_spec, lag_spec, mixed_spec, gates)
    result = exchange(result, "seq", middle_first(seq_count))

    lag_width = width // chan_count
    grad_out, *lags = call(
        unpack,
        [struct((1, rows, width), BF16)] + [struct((lag_width, rows), F32)] * chan_count,
        [
            struct((seq_count, rows, 2 * unit), BF16),
            struct((width, rows), F32),
        ],
    )(*result)
    lags = exchange(lags, "chan", far_first(chan_count))
    (lag_grad,) = call(add_up, [struct((lag_width, rows), F32)])(*lags)
    return grad_out, lag_grad.T[None]


def solution(mesh):
    placed = (
        P("section", None, "seq", "chan"),
        P("section", None, "seq", "chan"),
        P("section", None, "seq", "chan"),
        P("section", "seq", "chan"),
        P("seq", "chan"),
        P("section", "seq", None),
        P("section", None),
    )

    def program(*args):
        return jax.shard_map(
            functools.partial(body, *transform_tables(args[0].shape[2])),
            mesh=mesh,
            in_specs=placed,
            out_specs=(P("section", "seq", "chan"), P("section", "seq", "chan")),
            check_vma=False,
        )(*args)

    return program
```

```python
import functools
import math

import jax
import jax.numpy as jnp
import ml_dtypes
import numpy as np
from jax import lax
from jax.experimental import pallas as pl
from jax.experimental.pallas import tpu as pltpu
from jax.sharding import PartitionSpec as P

BF16 = jnp.bfloat16
F32 = jnp.float32
HALF_TURN = math.sqrt(0.5)


def transform_tables(length):
    freq = np.concatenate([np.arange(rest, length, 4, dtype=np.int64) for rest in range(4)])
    position = np.arange(length // 2, dtype=np.int64)
    angles = math.pi / (2 * length) * ((2 * freq[:, None] + 1) * position[None, :] % (4 * length))
    table = np.concatenate([np.cos(angles), np.sin(angles)], axis=0).astype(ml_dtypes.bfloat16)
    return table, np.ascontiguousarray(table.T)


def size_of(shapes):
    total = 0
    for shape in shapes:
        lanes = -(-shape.shape[-1] // 128) * 128
        total += math.prod(shape.shape[:-1]) * lanes * jnp.dtype(shape.dtype).itemsize
    return total


def call(kernel, out_shape, scratch=(), spaces=None, copies=0):
    def run(*arrays):
        held = size_of([*arrays, *out_shape, *scratch])
        if spaces:
            arrays = [
                pltpu.with_memory_space_constraint(array, space) if space == pltpu.HBM else array
                for array, space in zip(arrays, spaces)
            ]
        scratch_shapes = [pltpu.VMEM(shape.shape, shape.dtype) for shape in scratch]
        if copies:
            scratch_shapes.append(pltpu.SemaphoreType.DMA((copies,)))
        return pl.pallas_call(
            kernel,
            out_shape=out_shape,
            in_specs=[
                pl.BlockSpec(memory_space=space)
                for space in spaces or [pltpu.VMEM] * len(arrays)
            ],
            scratch_shapes=scratch_shapes,
            compiler_params=pltpu.CompilerParams(vmem_limit_bytes=2 * held + (4 << 20)),
        )(*arrays)

    return run


def fetch(sources, places, semaphores):
    copies = [
        pltpu.make_async_copy(source, place, semaphores.at[at])
        for at, (source, place) in enumerate(zip(sources, places))
    ]
    for copy in copies:
        copy.start()
    return copies


def wait(copies):
    for copy in copies:
        copy.wait()


def dot(left, right):
    return jnp.dot(left, right, preferred_element_type=F32)


def pack(arrays, stage, outs):
    seq_index = lax.axis_index("seq")
    count = len(outs)
    unit = arrays[0].shape[1] // count
    for block in range(count):
        lanes = slice(block * unit, (block + 1) * unit)
        stage[block] = jnp.concatenate([array[:, lanes] for array in arrays], axis=1)
    for step, out in enumerate(outs):
        out[...] = stage[seq_index ^ step]


def pack_first(post, held, loss, pre, filters, *rest):
    *outs, stage, gates, lags, semaphores = rest
    sources = [post.at[0, 0], held.at[0], loss, pre.at[0, 0], filters.at[0]]
    wait(fetch(sources, [gates.at[at] for at in range(4)] + [lags], semaphores))
    gated = (gates[0].astype(F32) * gates[1].astype(F32)).astype(BF16)
    kept = jnp.where(lax.axis_index("section") == 0, gates[2], gates[1])
    pack([lags[...].astype(BF16), gated, gates[3], kept], stage, outs)


def pack_second(after, saved, pre, post, gains, forward, backward, *rest):
    del after
    *outs, gain, forward_out, backward_out, stage, gates, all_gains, semaphores = rest
    sources = [saved.at[0, 0], saved.at[0, 1], pre.at[0, 0], pre.at[0, 1], post.at[0, 1]]
    places = [gates.at[at] for at in range(5)]
    copies = fetch(
        [*sources, gains, forward, backward],
        [*places, all_gains, forward_out, backward_out],
        semaphores,
    )
    wait(copies[:6])
    mixed = (gates[0:2].astype(F32) * gates[2:4].astype(F32)).astype(BF16)
    pack([mixed[0], mixed[1], gates[4], gates[3]], stage, outs)
    unit = gain.shape[1] // 2
    for block in range(len(outs)):

        @pl.when(lax.axis_index("seq") == block)
        def _():
            own = all_gains[:, block * unit : (block + 1) * unit]
            gain[...] = jnp.concatenate([own, own], axis=1)

    wait(copies[6:])


def gather_positions(chunks, steps, held):
    seq_index = lax.axis_index("seq")
    rows = chunks[0].shape[0]
    for step, chunk in zip([0, *steps], chunks):
        at = pl.multiple_of((seq_index ^ step) * rows, rows)
        held[pl.ds(at, rows), :] = chunk[...]


def swap(array):
    unit = array.shape[1] // 2
    return jnp.concatenate([array[:, unit:], array[:, :unit]], axis=1)


def first_unit(array):
    return lax.broadcasted_iota(jnp.int32, array.shape, 1) < array.shape[1] // 2


def quarters(*arrays):
    size = arrays[0].shape[0] // 4
    return jnp.concatenate(
        [array[at * size : (at + 1) * size] for at, array in enumerate(arrays)], axis=0
    )


def spectrum(forward, top, bottom):
    both = dot(forward[...], jnp.concatenate([top, bottom], axis=1))
    length, lanes = both.shape[0] // 2, top.shape[1]
    real, imag = both[:length, lanes:], both[length:, lanes:]
    plus, minus = (real + imag) * HALF_TURN, (real - imag) * HALF_TURN
    return (
        both[:length, :lanes] + quarters(minus, -plus, -minus, plus),
        both[length:, :lanes] + quarters(plus, minus, -plus, -minus),
    )


def inverse(backward, real, imag):
    plus, minus = (real + imag) * HALF_TURN, (real - imag) * HALF_TURN
    real = jnp.concatenate([real, quarters(plus, -minus, -plus, minus)], axis=1)
    imag = jnp.concatenate([imag, quarters(-minus, -plus, minus, plus)], axis=1)
    return dot(backward[...], jnp.concatenate([real, imag], axis=0).astype(BF16))


def times_conj(real, imag, other_real, other_imag):
    return real * other_real + imag * other_imag, imag * other_real - real * other_imag


def halves(array):
    size, lanes = array.shape[0] // 2, array.shape[1] // 2
    return [
        (array[part * size : (part + 1) * size, :lanes], array[part * size : (part + 1) * size, lanes:])
        for part in range(2)
    ]


def first_tick(gain, forward, backward, *rest):
    *chunks, out, spectra, held = rest
    gather_positions(chunks, middle_first(len(chunks)), held)
    length, lanes = held.shape[0], gain.shape[1]
    parts = halves(held)
    real, imag = spectrum(forward, parts[0][0], parts[1][0])
    spectra[0], spectra[1] = real, imag
    both = inverse(backward, *times_conj(real, imag, swap(real), swap(imag))) * (1.0 / length)
    gradients = []
    for part, (first, second) in enumerate(parts):
        correlated = both[:, part * lanes : (part + 1) * lanes]
        kept = second.astype(F32)
        gradient = kept + swap(kept) * (correlated + gain[...] * first.astype(F32))
        gradients.append(jnp.where(lax.axis_index("section") == 0, kept, gradient))
    top, bottom = gradients
    out[...] = jnp.where(first_unit(top), swap(top), bottom).astype(BF16)


def mixed_spectra(scale, forward, spectra, *rest):
    *chunks, post, weight, other, lag_spec, held = rest
    gather_positions(chunks, near_first(len(chunks)), held)
    parts = halves(held)
    real, imag = spectrum(forward, parts[0][0], parts[1][0])
    low = first_unit(real)
    other[0] = jnp.where(low, spectra[0], real)
    other[1] = jnp.where(low, spectra[1], imag)
    lag_real, lag_imag = times_conj(spectra[0], spectra[1], swap(real), swap(imag))
    lag_spec[0] = jnp.where(low, 0.0, lag_real)
    lag_spec[1] = jnp.where(low, 0.0, lag_imag)
    for part, (_, gates) in enumerate(parts):
        gates = gates.astype(F32)
        low = first_unit(gates)
        post[part] = jnp.where(low, gates, swap(gates))
        weight[part] = jnp.where(low, swap(gates), scale)


def second_tick(gain, forward, backward, received, post, weight, other, lag_spec, *rest):
    *outs, stage = rest
    count, rows, lanes = stage.shape
    length = count * rows
    carried = received[...].astype(F32)
    low = first_unit(carried)
    carried = [jnp.where(low, carried, swap(carried)), jnp.where(low, swap(carried), carried)]
    gated = [(post[part] * carried[part]).astype(BF16) for part in range(2)]
    real, imag = times_conj(*spectrum(forward, *gated), other[0], other[1])
    both = inverse(backward, real + lag_spec[0], imag + lag_spec[1]) * (1.0 / length)
    for part in range(2):
        skipped = jnp.where(low, gain[...] * gated[part].astype(F32), 0.0)
        result = weight[part] * (both[:, part * lanes : (part + 1) * lanes] + skipped)
        result = jnp.where(low, carried[part] + result, result).astype(BF16)
        for block in range(count // 2):
            stage[part * (count // 2) + block] = result[block * rows : (block + 1) * rows]
    for step, out in enumerate(outs):
        out[...] = stage[lax.axis_index("seq") ^ step]


def unpack_gradient(*rest):
    *chunks, grad, stage = rest
    count = stage.shape[0]
    unit = stage.shape[2] // 2
    seq_index = lax.axis_index("seq")
    for step, chunk in zip([0, *middle_first(count)], chunks):
        stage[seq_index ^ step] = chunk[...]
    grad[0] = jnp.concatenate([stage[block][:, :unit] for block in range(count)], axis=1)


def unpack_lags(*rest):
    *refs, stage, lag_stage = rest
    count = stage.shape[0]
    chunks, lags = refs[:count], refs[count:]
    unit = stage.shape[2] // 2
    seq_index, chan_index = lax.axis_index("seq"), lax.axis_index("chan")
    for step, chunk in zip([0, *middle_first(count)], chunks):
        stage[seq_index ^ step] = chunk[...]
    lag_grad = jnp.concatenate([stage[block][:, unit:] for block in range(count)], axis=1)
    lag_stage[...] = lag_grad.astype(F32).T
    for step, lag in enumerate(lags):
        width = lag.shape[0]
        lag[...] = lag_stage[pl.ds(pl.multiple_of((chan_index ^ step) * width, width), width), :]


def add_up(*refs):
    *lags, out = refs
    out[...] = functools.reduce(jnp.add, [lag[...] for lag in lags])


def exchange(chunks, axis, steps):
    size = lax.axis_size(axis)
    return [chunks[0]] + [
        lax.ppermute(chunks[step], axis, [(i, i ^ step) for i in range(size)]) for step in steps
    ]


def middle_first(size):
    return [*range(2, size), 1]


def near_first(size):
    return list(range(1, size))


def far_first(size):
    return list(reversed(range(1, size)))


def body(forward, backward, *args):
    saved_input, pre_gate, post_gate, grad_held, loss_grad, filters, skip_gain = args
    seq_count = lax.axis_size("seq")
    chan_count = lax.axis_size("chan")
    section_count = lax.axis_size("section")
    _, tick_count, rows, width = saved_input.shape
    length = rows * seq_count
    unit = width // seq_count
    forward, backward = jnp.asarray(forward), jnp.asarray(backward)
    scale = 1.0 / math.sqrt(length * chan_count * tick_count)
    struct = jax.ShapeDtypeStruct
    chunk = struct((rows, 4 * unit), BF16)
    stage = struct((seq_count, rows, 4 * unit), BF16)
    held_rows = struct((length, 4 * unit), BF16)
    two_spectra = struct((2, length, 2 * unit), F32)
    two_parts = struct((2, length // 2, 2 * unit), F32)

    first = call(
        pack_first,
        [chunk] * seq_count,
        [stage, struct((4, rows, width), BF16), struct((rows, width), F32)],
        [pltpu.HBM] * 5,
        5,
    )(post_gate, grad_held, loss_grad, pre_gate, filters)
    *second, gain, forward, backward = call(
        pack_second,
        [chunk] * seq_count
        + [
            struct((1, 2 * unit), F32),
            struct(forward.shape, BF16),
            struct(backward.shape, BF16),
        ],
        [stage, struct((5, rows, width), BF16), struct((1, width), F32)],
        [pl.ANY] + [pltpu.HBM] * 6,
        8,
    )(first[0], saved_input, pre_gate, post_gate, skip_gain, forward, backward)
    first = exchange(first, "seq", middle_first(seq_count))
    second = exchange(second, "seq", near_first(seq_count))

    gradient, spectra = call(
        first_tick,
        [struct((length // 2, 2 * unit), BF16), two_spectra],
        [held_rows],
    )(gain, forward, backward, *first)
    ring = [(i, (i - 1) % section_count) for i in range(section_count)]
    received = lax.ppermute(gradient, "section", ring)

    prepared = call(
        functools.partial(mixed_spectra, scale),
        [two_parts, two_parts, two_spectra, two_spectra],
        [held_rows],
    )(forward, spectra, *second)

    sorted_chunks = struct((seq_count, rows, 2 * unit), BF16)
    result = call(
        second_tick,
        [struct((rows, 2 * unit), BF16)] * seq_count,
        [sorted_chunks],
    )(gain, forward, backward, received, *prepared)
    result = exchange(result, "seq", middle_first(seq_count))

    lag_width = width // chan_count
    lags = call(
        unpack_lags,
        [struct((lag_width, rows), F32)] * chan_count,
        [sorted_chunks, struct((width, rows), F32)],
    )(*result)
    lags = exchange(lags, "chan", far_first(chan_count))
    (grad_out,) = call(unpack_gradient, [struct((1, rows, width), BF16)], [sorted_chunks])(*result)
    (lag_grad,) = call(add_up, [struct((lag_width, rows), F32)])(*lags)
    return grad_out, lag_grad.T[None]


def solution(mesh):
    placed = (
        P("section", None, "seq", "chan"),
        P("section", None, "seq", "chan"),
        P("section", None, "seq", "chan"),
        P("section", "seq", "chan"),
        P("seq", "chan"),
        P("section", "seq", None),
        P("section", None),
    )

    def program(*args):
        return jax.shard_map(
            functools.partial(body, *transform_tables(args[0].shape[2])),
            mesh=mesh,
            in_specs=placed,
            out_specs=(P("section", "seq", "chan"), P("section", "seq", "chan")),
            check_vma=False,
        )(*args)

    return program
```

```python
import functools
import math

import jax
import jax.numpy as jnp
import ml_dtypes
import numpy as np
from jax import lax
from jax.experimental import pallas as pl
from jax.experimental.pallas import tpu as pltpu
from jax.sharding import PartitionSpec as P

BF16 = jnp.bfloat16
F32 = jnp.float32
HALF_TURN = math.sqrt(0.5)


def transform_tables(length):
    freq = np.concatenate([np.arange(rest, length, 4, dtype=np.int64) for rest in range(4)])
    position = np.arange(length // 2, dtype=np.int64)
    angles = math.pi / (2 * length) * ((2 * freq[:, None] + 1) * position[None, :] % (4 * length))
    table = np.concatenate([np.cos(angles), np.sin(angles)], axis=0).astype(ml_dtypes.bfloat16)
    return table, np.ascontiguousarray(table.T)


def size_of(shapes):
    total = 0
    for shape in shapes:
        lanes = -(-shape.shape[-1] // 128) * 128
        total += math.prod(shape.shape[:-1]) * lanes * jnp.dtype(shape.dtype).itemsize
    return total


def call(kernel, out_shape, scratch=(), spaces=None, copies=0):
    def run(*arrays):
        held = size_of([*arrays, *out_shape, *scratch])
        if spaces:
            arrays = [
                pltpu.with_memory_space_constraint(array, space) if space == pltpu.HBM else array
                for array, space in zip(arrays, spaces)
            ]
        scratch_shapes = [pltpu.VMEM(shape.shape, shape.dtype) for shape in scratch]
        if copies:
            scratch_shapes.append(pltpu.SemaphoreType.DMA((copies,)))
        return pl.pallas_call(
            kernel,
            out_shape=out_shape,
            in_specs=[
                pl.BlockSpec(memory_space=space)
                for space in spaces or [pltpu.VMEM] * len(arrays)
            ],
            scratch_shapes=scratch_shapes,
            compiler_params=pltpu.CompilerParams(vmem_limit_bytes=2 * held + (4 << 20)),
        )(*arrays)

    return run


def fetch(sources, places, semaphores):
    copies = [
        pltpu.make_async_copy(source, place, semaphores.at[at])
        for at, (source, place) in enumerate(zip(sources, places))
    ]
    for copy in copies:
        copy.start()
    return copies


def wait(copies):
    for copy in copies:
        copy.wait()


def dot(left, right):
    return jnp.dot(left, right, preferred_element_type=F32)


def pack(arrays, stage, outs):
    seq_index = lax.axis_index("seq")
    count = len(outs)
    unit = arrays[0].shape[1] // count
    for block in range(count):
        lanes = slice(block * unit, (block + 1) * unit)
        stage[block] = jnp.concatenate([array[:, lanes] for array in arrays], axis=1)
    for step, out in enumerate(outs):
        out[...] = stage[seq_index ^ step]


def pack_first(post, held, loss, pre, filters, *rest):
    *outs, stage, gates, lags, semaphores = rest
    sources = [post.at[0, 0], held.at[0], loss, pre.at[0, 0], filters.at[0]]
    wait(fetch(sources, [gates.at[at] for at in range(4)] + [lags], semaphores))
    gated = (gates[0].astype(F32) * gates[1].astype(F32)).astype(BF16)
    kept = jnp.where(lax.axis_index("section") == 0, gates[2], gates[1])
    pack([lags[...].astype(BF16), gated, gates[3], kept], stage, outs)


def pack_second(after, saved, pre, post, gains, forward, backward, *rest):
    del after
    *outs, gain, forward_out, backward_out, stage, gates, all_gains, semaphores = rest
    sources = [saved.at[0, 0], saved.at[0, 1], pre.at[0, 0], pre.at[0, 1], post.at[0, 1]]
    places = [gates.at[at] for at in range(5)]
    copies = fetch(
        [*sources, gains, forward, backward],
        [*places, all_gains, forward_out, backward_out],
        semaphores,
    )
    wait(copies[:6])
    mixed = (gates[0:2].astype(F32) * gates[2:4].astype(F32)).astype(BF16)
    pack([mixed[0], mixed[1], gates[4], gates[3]], stage, outs)
    unit = gain.shape[1] // 2
    for block in range(len(outs)):

        @pl.when(lax.axis_index("seq") == block)
        def _():
            own = all_gains[:, block * unit : (block + 1) * unit]
            gain[...] = jnp.concatenate([own, own], axis=1)

    wait(copies[6:])


def gather_positions(chunks, steps, held):
    seq_index = lax.axis_index("seq")
    rows = chunks[0].shape[0]
    for step, chunk in zip([0, *steps], chunks):
        at = pl.multiple_of((seq_index ^ step) * rows, rows)
        held[pl.ds(at, rows), :] = chunk[...]


def swap(array):
    unit = array.shape[1] // 2
    return jnp.concatenate([array[:, unit:], array[:, :unit]], axis=1)


def first_unit(array):
    return lax.broadcasted_iota(jnp.int32, array.shape, 1) < array.shape[1] // 2


def quarters(*arrays):
    size = arrays[0].shape[0] // 4
    return jnp.concatenate(
        [array[at * size : (at + 1) * size] for at, array in enumerate(arrays)], axis=0
    )


def spectrum(forward, top, bottom):
    both = dot(forward[...], jnp.concatenate([top, bottom], axis=1))
    length, lanes = both.shape[0] // 2, top.shape[1]
    real, imag = both[:length, lanes:], both[length:, lanes:]
    plus, minus = (real + imag) * HALF_TURN, (real - imag) * HALF_TURN
    return (
        both[:length, :lanes] + quarters(minus, -plus, -minus, plus),
        both[length:, :lanes] + quarters(plus, minus, -plus, -minus),
    )


def inverse(backward, real, imag):
    plus, minus = (real + imag) * HALF_TURN, (real - imag) * HALF_TURN
    real = jnp.concatenate([real, quarters(plus, -minus, -plus, minus)], axis=1)
    imag = jnp.concatenate([imag, quarters(-minus, -plus, minus, plus)], axis=1)
    return dot(backward[...], jnp.concatenate([real, imag], axis=0).astype(BF16))


def times_conj(real, imag, other_real, other_imag):
    return real * other_real + imag * other_imag, imag * other_real - real * other_imag


def halves(array):
    size, lanes = array.shape[0] // 2, array.shape[1] // 2
    return [
        (array[part * size : (part + 1) * size, :lanes], array[part * size : (part + 1) * size, lanes:])
        for part in range(2)
    ]


def first_tick(gain, forward, backward, *rest):
    *chunks, out, spectra, held = rest
    gather_positions(chunks, middle_first(len(chunks)), held)
    length, lanes = held.shape[0], gain.shape[1]
    parts = halves(held)
    real, imag = spectrum(forward, parts[0][0], parts[1][0])
    spectra[0], spectra[1] = real, imag
    both = inverse(backward, *times_conj(real, imag, swap(real), swap(imag))) * (1.0 / length)
    gradients = []
    for part, (first, second) in enumerate(parts):
        correlated = both[:, part * lanes : (part + 1) * lanes]
        kept = second.astype(F32)
        gradient = kept + swap(kept) * (correlated + gain[...] * first.astype(F32))
        gradients.append(jnp.where(lax.axis_index("section") == 0, kept, gradient))
    top, bottom = gradients
    out[...] = jnp.where(first_unit(top), swap(top), bottom).astype(BF16)


def mixed_spectra(scale, forward, spectra, *rest):
    *chunks, post, weight, other, lag_spec, held = rest
    gather_positions(chunks, near_first(len(chunks)), held)
    parts = halves(held)
    real, imag = spectrum(forward, parts[0][0], parts[1][0])
    low = first_unit(real)
    other[0] = jnp.where(low, spectra[0], real)
    other[1] = jnp.where(low, spectra[1], imag)
    lag_real, lag_imag = times_conj(spectra[0], spectra[1], swap(real), swap(imag))
    lag_spec[0] = jnp.where(low, 0.0, lag_real)
    lag_spec[1] = jnp.where(low, 0.0, lag_imag)
    for part, (_, gates) in enumerate(parts):
        gates = gates.astype(F32)
        low = first_unit(gates)
        post[part] = jnp.where(low, gates, swap(gates))
        weight[part] = jnp.where(low, swap(gates), scale)


def second_tick(gain, forward, backward, received, post, weight, other, lag_spec, *rest):
    *outs, stage = rest
    count, rows, lanes = stage.shape
    length = count * rows
    carried = received[...].astype(F32)
    low = first_unit(carried)
    carried = [jnp.where(low, carried, swap(carried)), jnp.where(low, swap(carried), carried)]
    gated = [(post[part] * carried[part]).astype(BF16) for part in range(2)]
    real, imag = times_conj(*spectrum(forward, *gated), other[0], other[1])
    both = inverse(backward, real + lag_spec[0], imag + lag_spec[1]) * (1.0 / length)
    for part in range(2):
        skipped = jnp.where(low, gain[...] * gated[part].astype(F32), 0.0)
        result = weight[part] * (both[:, part * lanes : (part + 1) * lanes] + skipped)
        result = jnp.where(low, carried[part] + result, result).astype(BF16)
        for block in range(count // 2):
            stage[part * (count // 2) + block] = result[block * rows : (block + 1) * rows]
    for step, out in enumerate(outs):
        out[...] = stage[lax.axis_index("seq") ^ step]


def unpack_gradient(*rest):
    *chunks, grad, stage = rest
    count = stage.shape[0]
    unit = stage.shape[2] // 2
    seq_index = lax.axis_index("seq")
    for step, chunk in zip([0, *middle_first(count)], chunks):
        stage[seq_index ^ step] = chunk[...]
    grad[0] = jnp.concatenate([stage[block][:, :unit] for block in range(count)], axis=1)


def unpack_lags(*rest):
    *refs, stage, lag_stage = rest
    count = stage.shape[0]
    chunks, lags = refs[:count], refs[count:]
    unit = stage.shape[2] // 2
    seq_index, chan_index = lax.axis_index("seq"), lax.axis_index("chan")
    for step, chunk in zip([0, *middle_first(count)], chunks):
        stage[seq_index ^ step] = chunk[...]
    lag_grad = jnp.concatenate([stage[block][:, unit:] for block in range(count)], axis=1)
    lag_stage[...] = lag_grad.astype(F32).T.astype(BF16)
    for step, lag in enumerate(lags):
        width = lag.shape[0]
        lag[...] = lag_stage[pl.ds(pl.multiple_of((chan_index ^ step) * width, width), width), :]


def add_up(*refs):
    *lags, out = refs
    out[...] = functools.reduce(jnp.add, [lag[...].astype(F32) for lag in lags])


def exchange(chunks, axis, steps):
    size = lax.axis_size(axis)
    return [chunks[0]] + [
        lax.ppermute(chunks[step], axis, [(i, i ^ step) for i in range(size)]) for step in steps
    ]


def middle_first(size):
    return [*range(2, size), 1]


def near_first(size):
    return list(range(1, size))


def far_first(size):
    return list(reversed(range(1, size)))


def body(forward, backward, *args):
    saved_input, pre_gate, post_gate, grad_held, loss_grad, filters, skip_gain = args
    seq_count = lax.axis_size("seq")
    chan_count = lax.axis_size("chan")
    section_count = lax.axis_size("section")
    _, tick_count, rows, width = saved_input.shape
    length = rows * seq_count
    unit = width // seq_count
    forward, backward = jnp.asarray(forward), jnp.asarray(backward)
    scale = 1.0 / math.sqrt(length * chan_count * tick_count)
    struct = jax.ShapeDtypeStruct
    chunk = struct((rows, 4 * unit), BF16)
    stage = struct((seq_count, rows, 4 * unit), BF16)
    held_rows = struct((length, 4 * unit), BF16)
    two_spectra = struct((2, length, 2 * unit), F32)
    two_parts = struct((2, length // 2, 2 * unit), F32)

    first = call(
        pack_first,
        [chunk] * seq_count,
        [stage, struct((4, rows, width), BF16), struct((rows, width), F32)],
        [pltpu.HBM] * 5,
        5,
    )(post_gate, grad_held, loss_grad, pre_gate, filters)
    *second, gain, forward, backward = call(
        pack_second,
        [chunk] * seq_count
        + [
            struct((1, 2 * unit), F32),
            struct(forward.shape, BF16),
            struct(backward.shape, BF16),
        ],
        [stage, struct((5, rows, width), BF16), struct((1, width), F32)],
        [pl.ANY] + [pltpu.HBM] * 6,
        8,
    )(first[0], saved_input, pre_gate, post_gate, skip_gain, forward, backward)
    first = exchange(first, "seq", middle_first(seq_count))
    second = exchange(second, "seq", near_first(seq_count))

    gradient, spectra = call(
        first_tick,
        [struct((length // 2, 2 * unit), BF16), two_spectra],
        [held_rows],
    )(gain, forward, backward, *first)
    ring = [(i, (i - 1) % section_count) for i in range(section_count)]
    received = lax.ppermute(gradient, "section", ring)

    prepared = call(
        functools.partial(mixed_spectra, scale),
        [two_parts, two_parts, two_spectra, two_spectra],
        [held_rows],
    )(forward, spectra, *second)

    sorted_chunks = struct((seq_count, rows, 2 * unit), BF16)
    result = call(
        second_tick,
        [struct((rows, 2 * unit), BF16)] * seq_count,
        [sorted_chunks],
    )(gain, forward, backward, received, *prepared)
    result = exchange(result, "seq", middle_first(seq_count))

    lag_width = width // chan_count
    lags = call(
        unpack_lags,
        [struct((lag_width, rows), BF16)] * chan_count,
        [sorted_chunks, struct((width, rows), BF16)],
    )(*result)
    lags = exchange(lags, "chan", far_first(chan_count))
    (grad_out,) = call(unpack_gradient, [struct((1, rows, width), BF16)], [sorted_chunks])(*result)
    (lag_grad,) = call(add_up, [struct((lag_width, rows), F32)])(*lags)
    return grad_out, lag_grad.T[None]


def solution(mesh):
    placed = (
        P("section", None, "seq", "chan"),
        P("section", None, "seq", "chan"),
        P("section", None, "seq", "chan"),
        P("section", "seq", "chan"),
        P("seq", "chan"),
        P("section", "seq", None),
        P("section", None),
    )

    def program(*args):
        return jax.shard_map(
            functools.partial(body, *transform_tables(args[0].shape[2])),
            mesh=mesh,
            in_specs=placed,
            out_specs=(P("section", "seq", "chan"), P("section", "seq", "chan")),
            check_vma=False,
        )(*args)

    return program
```

```python
import functools
import math

import jax
import jax.numpy as jnp
import ml_dtypes
import numpy as np
from jax import lax
from jax.experimental import pallas as pl
from jax.experimental.pallas import tpu as pltpu
from jax.sharding import PartitionSpec as P

BF16 = jnp.bfloat16
F32 = jnp.float32
HALF_TURN = math.sqrt(0.5)


def transform_tables(length):
    freq = np.concatenate([np.arange(rest, length, 4, dtype=np.int64) for rest in range(4)])
    position = np.arange(length // 2, dtype=np.int64)
    angles = math.pi / (2 * length) * ((2 * freq[:, None] + 1) * position[None, :] % (4 * length))
    table = np.concatenate([np.cos(angles), np.sin(angles)], axis=0).astype(ml_dtypes.bfloat16)
    return table, np.ascontiguousarray(table.T)


def size_of(shapes):
    total = 0
    for shape in shapes:
        lanes = -(-shape.shape[-1] // 128) * 128
        total += math.prod(shape.shape[:-1]) * lanes * jnp.dtype(shape.dtype).itemsize
    return total


def call(kernel, out_shape, scratch=(), spaces=None, copies=0):
    def run(*arrays):
        held = size_of([*arrays, *out_shape, *scratch])
        if spaces:
            arrays = [
                pltpu.with_memory_space_constraint(array, space) if space == pltpu.HBM else array
                for array, space in zip(arrays, spaces)
            ]
        scratch_shapes = [pltpu.VMEM(shape.shape, shape.dtype) for shape in scratch]
        if copies:
            scratch_shapes.append(pltpu.SemaphoreType.DMA((copies,)))
        return pl.pallas_call(
            kernel,
            out_shape=out_shape,
            in_specs=[
                pl.BlockSpec(memory_space=space)
                for space in spaces or [pltpu.VMEM] * len(arrays)
            ],
            scratch_shapes=scratch_shapes,
            compiler_params=pltpu.CompilerParams(vmem_limit_bytes=2 * held + (4 << 20)),
        )(*arrays)

    return run


def fetch(sources, places, semaphores):
    copies = [
        pltpu.make_async_copy(source, place, semaphores.at[at])
        for at, (source, place) in enumerate(zip(sources, places))
    ]
    for copy in copies:
        copy.start()
    return copies


def wait(copies):
    for copy in copies:
        copy.wait()


def dot(left, right):
    return jnp.dot(left, right, preferred_element_type=F32)


def pack(arrays, stage, outs):
    seq_index = lax.axis_index("seq")
    count = len(outs)
    unit = arrays[0].shape[1] // count
    for block in range(count):
        lanes = slice(block * unit, (block + 1) * unit)
        stage[block] = jnp.concatenate([array[:, lanes] for array in arrays], axis=1)
    for step, out in enumerate(outs):
        out[...] = stage[seq_index ^ step]


def pack_first(post, held, loss, pre, filters, *rest):
    *outs, stage, gates, lags, semaphores = rest
    sources = [post.at[0, 0], held.at[0], loss, pre.at[0, 0], filters.at[0]]
    wait(fetch(sources, [gates.at[at] for at in range(4)] + [lags], semaphores))
    gated = (gates[0].astype(F32) * gates[1].astype(F32)).astype(BF16)
    kept = jnp.where(lax.axis_index("section") == 0, gates[2], gates[1])
    pack([lags[...].astype(BF16), gated, gates[3], kept], stage, outs)


def pack_second(after, saved, pre, post, gains, forward, backward, *rest):
    del after
    *outs, gain, forward_out, backward_out, stage, gates, all_gains, semaphores = rest
    sources = [saved.at[0, 0], saved.at[0, 1], pre.at[0, 0], pre.at[0, 1], post.at[0, 1]]
    places = [gates.at[at] for at in range(5)]
    copies = fetch(
        [*sources, gains, forward, backward],
        [*places, all_gains, forward_out, backward_out],
        semaphores,
    )
    wait(copies[:6])
    mixed = (gates[0:2].astype(F32) * gates[2:4].astype(F32)).astype(BF16)
    pack([mixed[0], mixed[1], gates[4], gates[3]], stage, outs)
    unit = gain.shape[1] // 2
    for block in range(len(outs)):

        @pl.when(lax.axis_index("seq") == block)
        def _():
            own = all_gains[:, block * unit : (block + 1) * unit]
            gain[...] = jnp.concatenate([own, own], axis=1)

    wait(copies[6:])


def gather_positions(chunks, steps, held):
    seq_index = lax.axis_index("seq")
    rows = chunks[0].shape[0]
    for step, chunk in zip([0, *steps], chunks):
        at = pl.multiple_of((seq_index ^ step) * rows, rows)
        held[pl.ds(at, rows), :] = chunk[...]


def swap(array):
    unit = array.shape[1] // 2
    return jnp.concatenate([array[:, unit:], array[:, :unit]], axis=1)


def first_unit(array):
    return lax.broadcasted_iota(jnp.int32, array.shape, 1) < array.shape[1] // 2


def quarters(*arrays):
    size = arrays[0].shape[0] // 4
    return jnp.concatenate(
        [array[at * size : (at + 1) * size] for at, array in enumerate(arrays)], axis=0
    )


def spectrum(forward, top, bottom):
    both = dot(forward[...], jnp.concatenate([top, bottom], axis=1))
    length, lanes = both.shape[0] // 2, top.shape[1]
    real, imag = both[:length, lanes:], both[length:, lanes:]
    plus, minus = (real + imag) * HALF_TURN, (real - imag) * HALF_TURN
    return (
        both[:length, :lanes] + quarters(minus, -plus, -minus, plus),
        both[length:, :lanes] + quarters(plus, minus, -plus, -minus),
    )


def inverse(backward, real, imag):
    plus, minus = (real + imag) * HALF_TURN, (real - imag) * HALF_TURN
    real = jnp.concatenate([real, quarters(plus, -minus, -plus, minus)], axis=1)
    imag = jnp.concatenate([imag, quarters(-minus, -plus, minus, plus)], axis=1)
    return dot(backward[...], jnp.concatenate([real, imag], axis=0).astype(BF16))


def times_conj(real, imag, other_real, other_imag):
    return real * other_real + imag * other_imag, imag * other_real - real * other_imag


def halves(array):
    size, lanes = array.shape[0] // 2, array.shape[1] // 2
    return [
        (array[part * size : (part + 1) * size, :lanes], array[part * size : (part + 1) * size, lanes:])
        for part in range(2)
    ]


def first_tick(gain, forward, backward, *rest):
    *chunks, out, spectra, held = rest
    gather_positions(chunks, middle_first(len(chunks)), held)
    length, lanes = held.shape[0], gain.shape[1]
    parts = halves(held)
    real, imag = spectrum(forward, parts[0][0], parts[1][0])
    spectra[0], spectra[1] = real, imag
    both = inverse(backward, *times_conj(real, imag, swap(real), swap(imag))) * (1.0 / length)
    gradients = []
    for part, (first, second) in enumerate(parts):
        correlated = both[:, part * lanes : (part + 1) * lanes]
        kept = second.astype(F32)
        gradient = kept + swap(kept) * (correlated + gain[...] * first.astype(F32))
        gradients.append(jnp.where(lax.axis_index("section") == 0, kept, gradient))
    top, bottom = gradients
    out[...] = jnp.where(first_unit(top), swap(top), bottom).astype(BF16)


def mixed_spectra(scale, forward, spectra, *rest):
    *chunks, post, weight, other, lag_spec, held = rest
    gather_positions(chunks, near_first(len(chunks)), held)
    parts = halves(held)
    real, imag = spectrum(forward, parts[0][0], parts[1][0])
    low = first_unit(real)
    other[0] = jnp.where(low, spectra[0], real)
    other[1] = jnp.where(low, spectra[1], imag)
    lag_real, lag_imag = times_conj(spectra[0], spectra[1], swap(real), swap(imag))
    lag_spec[0] = jnp.where(low, 0.0, lag_real)
    lag_spec[1] = jnp.where(low, 0.0, lag_imag)
    for part, (_, gates) in enumerate(parts):
        gates = gates.astype(F32)
        low = first_unit(gates)
        post[part] = jnp.where(low, gates, swap(gates))
        weight[part] = jnp.where(low, swap(gates), scale)


def second_tick(gain, forward, backward, received, post, weight, other, lag_spec, *rest):
    *outs, stage = rest
    count, rows, lanes = stage.shape
    length = count * rows
    carried = received[...].astype(F32)
    low = first_unit(carried)
    carried = [jnp.where(low, carried, swap(carried)), jnp.where(low, swap(carried), carried)]
    gated = [(post[part] * carried[part]).astype(BF16) for part in range(2)]
    real, imag = times_conj(*spectrum(forward, *gated), other[0], other[1])
    both = inverse(backward, real + lag_spec[0], imag + lag_spec[1]) * (1.0 / length)
    for part in range(2):
        skipped = jnp.where(low, gain[...] * gated[part].astype(F32), 0.0)
        result = weight[part] * (both[:, part * lanes : (part + 1) * lanes] + skipped)
        result = jnp.where(low, carried[part] + result, result).astype(BF16)
        for block in range(count // 2):
            stage[part * (count // 2) + block] = result[block * rows : (block + 1) * rows]
    for step, out in enumerate(outs):
        out[...] = stage[lax.axis_index("seq") ^ step]


def unpack_gradient(*rest):
    *chunks, grad, stage = rest
    count = stage.shape[0]
    unit = stage.shape[2] // 2
    seq_index = lax.axis_index("seq")
    for step, chunk in zip([0, *farthest_first(count)], chunks):
        stage[seq_index ^ step] = chunk[...]
    grad[0] = jnp.concatenate([stage[block][:, :unit] for block in range(count)], axis=1)


def unpack_lags(*rest):
    *refs, stage, lag_stage = rest
    count = stage.shape[0]
    chunks, lags = refs[:count], refs[count:]
    unit = stage.shape[2] // 2
    seq_index, chan_index = lax.axis_index("seq"), lax.axis_index("chan")
    for step, chunk in zip([0, *farthest_first(count)], chunks):
        stage[seq_index ^ step] = chunk[...]
    lag_grad = jnp.concatenate([stage[block][:, unit:] for block in range(count)], axis=1)
    lag_stage[...] = lag_grad.astype(F32).T.astype(BF16)
    for step, lag in enumerate(lags):
        width = lag.shape[0]
        lag[...] = lag_stage[pl.ds(pl.multiple_of((chan_index ^ step) * width, width), width), :]


def add_up(*refs):
    *lags, out = refs
    out[...] = functools.reduce(jnp.add, [lag[...].astype(F32) for lag in lags])


def exchange(chunks, axis, steps):
    size = lax.axis_size(axis)
    return [chunks[0]] + [
        lax.ppermute(chunks[step], axis, [(i, i ^ step) for i in range(size)]) for step in steps
    ]


def middle_first(size):
    return [*range(2, size), 1]


def farthest_first(size):
    return [size - 1, *range(1, size - 1)]


def near_first(size):
    return list(range(1, size))


def far_first(size):
    return list(reversed(range(1, size)))


def body(forward, backward, *args):
    saved_input, pre_gate, post_gate, grad_held, loss_grad, filters, skip_gain = args
    seq_count = lax.axis_size("seq")
    chan_count = lax.axis_size("chan")
    section_count = lax.axis_size("section")
    _, tick_count, rows, width = saved_input.shape
    length = rows * seq_count
    unit = width // seq_count
    forward, backward = jnp.asarray(forward), jnp.asarray(backward)
    scale = 1.0 / math.sqrt(length * chan_count * tick_count)
    struct = jax.ShapeDtypeStruct
    chunk = struct((rows, 4 * unit), BF16)
    stage = struct((seq_count, rows, 4 * unit), BF16)
    held_rows = struct((length, 4 * unit), BF16)
    two_spectra = struct((2, length, 2 * unit), F32)
    two_parts = struct((2, length // 2, 2 * unit), F32)

    first = call(
        pack_first,
        [chunk] * seq_count,
        [stage, struct((4, rows, width), BF16), struct((rows, width), F32)],
        [pltpu.HBM] * 5,
        5,
    )(post_gate, grad_held, loss_grad, pre_gate, filters)
    *second, gain, forward, backward = call(
        pack_second,
        [chunk] * seq_count
        + [
            struct((1, 2 * unit), F32),
            struct(forward.shape, BF16),
            struct(backward.shape, BF16),
        ],
        [stage, struct((5, rows, width), BF16), struct((1, width), F32)],
        [pl.ANY] + [pltpu.HBM] * 6,
        8,
    )(first[0], saved_input, pre_gate, post_gate, skip_gain, forward, backward)
    first = exchange(first, "seq", middle_first(seq_count))
    second = exchange(second, "seq", near_first(seq_count))

    gradient, spectra = call(
        first_tick,
        [struct((length // 2, 2 * unit), BF16), two_spectra],
        [held_rows],
    )(gain, forward, backward, *first)
    ring = [(i, (i - 1) % section_count) for i in range(section_count)]
    received = lax.ppermute(gradient, "section", ring)

    prepared = call(
        functools.partial(mixed_spectra, scale),
        [two_parts, two_parts, two_spectra, two_spectra],
        [held_rows],
    )(forward, spectra, *second)

    sorted_chunks = struct((seq_count, rows, 2 * unit), BF16)
    result = call(
        second_tick,
        [struct((rows, 2 * unit), BF16)] * seq_count,
        [sorted_chunks],
    )(gain, forward, backward, received, *prepared)
    result = exchange(result, "seq", farthest_first(seq_count))

    lag_width = width // chan_count
    lags = call(
        unpack_lags,
        [struct((lag_width, rows), BF16)] * chan_count,
        [sorted_chunks, struct((width, rows), BF16)],
    )(*result)
    lags = exchange(lags, "chan", far_first(chan_count))
    (grad_out,) = call(unpack_gradient, [struct((1, rows, width), BF16)], [sorted_chunks])(*result)
    (lag_grad,) = call(add_up, [struct((lag_width, rows), F32)])(*lags)
    return grad_out, lag_grad.T[None]


def solution(mesh):
    placed = (
        P("section", None, "seq", "chan"),
        P("section", None, "seq", "chan"),
        P("section", None, "seq", "chan"),
        P("section", "seq", "chan"),
        P("seq", "chan"),
        P("section", "seq", None),
        P("section", None),
    )

    def program(*args):
        return jax.shard_map(
            functools.partial(body, *transform_tables(args[0].shape[2])),
            mesh=mesh,
            in_specs=placed,
            out_specs=(P("section", "seq", "chan"), P("section", "seq", "chan")),
            check_vma=False,
        )(*args)

    return program
```

```python
import functools
import math

import jax
import jax.numpy as jnp
import ml_dtypes
import numpy as np
from jax import lax
from jax.experimental import pallas as pl
from jax.experimental.pallas import tpu as pltpu
from jax.sharding import PartitionSpec as P

BF16 = jnp.bfloat16
F32 = jnp.float32
HALF_TURN = math.sqrt(0.5)
OWN = (0, 0)


def both(steps):
    return [(step, step) for step in steps]


def first_steps(size):
    return both([*range(2, size), 1])


def second_steps(size):
    near = list(range(1, size))
    return list(zip(near, [*near[1::-1], *near[2:]]))


def last_steps(size):
    return both([size - 1, *range(1, size - 1)])


def transform_tables(length):
    freq = np.concatenate([np.arange(rest, length, 4, dtype=np.int64) for rest in range(4)])
    position = np.arange(length // 2, dtype=np.int64)
    angles = math.pi / (2 * length) * ((2 * freq[:, None] + 1) * position[None, :] % (4 * length))
    table = np.concatenate([np.cos(angles), np.sin(angles)], axis=0).astype(ml_dtypes.bfloat16)
    return table, np.ascontiguousarray(table.T)


def size_of(shapes):
    total = 0
    for shape in shapes:
        lanes = -(-shape.shape[-1] // 128) * 128
        total += math.prod(shape.shape[:-1]) * lanes * jnp.dtype(shape.dtype).itemsize
    return total


def call(kernel, out_shape, scratch=(), spaces=None, copies=0):
    def run(*arrays):
        held = size_of([*arrays, *out_shape, *scratch])
        if spaces:
            arrays = [
                pltpu.with_memory_space_constraint(array, space) if space == pltpu.HBM else array
                for array, space in zip(arrays, spaces)
            ]
        scratch_shapes = [pltpu.VMEM(shape.shape, shape.dtype) for shape in scratch]
        if copies:
            scratch_shapes.append(pltpu.SemaphoreType.DMA((copies,)))
        return pl.pallas_call(
            kernel,
            out_shape=out_shape,
            in_specs=[
                pl.BlockSpec(memory_space=space)
                for space in spaces or [pltpu.VMEM] * len(arrays)
            ],
            scratch_shapes=scratch_shapes,
            compiler_params=pltpu.CompilerParams(vmem_limit_bytes=2 * held + (4 << 20)),
        )(*arrays)

    return run


def fetch(sources, places, semaphores):
    copies = [
        pltpu.make_async_copy(source, place, semaphores.at[at])
        for at, (source, place) in enumerate(zip(sources, places))
    ]
    for copy in copies:
        copy.start()
    return copies


def wait(copies):
    for copy in copies:
        copy.wait()


def dot(left, right):
    return jnp.dot(left, right, preferred_element_type=F32)


def place(step):
    even, odd = step
    return lax.axis_index("seq") ^ jnp.where(lax.axis_index("section") % 2 == 0, even, odd)


def pack(arrays, stage, outs, steps):
    count = len(outs)
    unit = arrays[0].shape[1] // count
    for block in range(count):
        lanes = slice(block * unit, (block + 1) * unit)
        stage[block] = jnp.concatenate([array[:, lanes] for array in arrays], axis=1)
    for step, out in zip([OWN, *steps], outs):
        out[...] = stage[place(step)]


def pack_first(post, held, loss, pre, filters, *rest):
    *outs, stage, gates, lags, semaphores = rest
    sources = [post.at[0, 0], held.at[0], loss, pre.at[0, 0], filters.at[0]]
    wait(fetch(sources, [gates.at[at] for at in range(4)] + [lags], semaphores))
    gated = (gates[0].astype(F32) * gates[1].astype(F32)).astype(BF16)
    kept = jnp.where(lax.axis_index("section") == 0, gates[2], gates[1])
    pack([lags[...].astype(BF16), gated, gates[3], kept], stage, outs, first_steps(len(outs)))


def pack_second(after, saved, pre, post, gains, forward, backward, *rest):
    del after
    *outs, gain, forward_out, backward_out, stage, gates, all_gains, semaphores = rest
    sources = [saved.at[0, 0], saved.at[0, 1], pre.at[0, 0], pre.at[0, 1], post.at[0, 1]]
    places = [gates.at[at] for at in range(5)]
    copies = fetch(
        [*sources, gains, forward, backward],
        [*places, all_gains, forward_out, backward_out],
        semaphores,
    )
    wait(copies[:6])
    mixed = (gates[0:2].astype(F32) * gates[2:4].astype(F32)).astype(BF16)
    pack([mixed[0], mixed[1], gates[4], gates[3]], stage, outs, second_steps(len(outs)))
    unit = gain.shape[1] // 2
    for block in range(len(outs)):

        @pl.when(lax.axis_index("seq") == block)
        def _():
            own = all_gains[:, block * unit : (block + 1) * unit]
            gain[...] = jnp.concatenate([own, own], axis=1)

    wait(copies[6:])


def gather_positions(chunks, steps, held):
    rows = chunks[0].shape[0]
    for step, chunk in zip([OWN, *steps], chunks):
        at = pl.multiple_of(place(step) * rows, rows)
        held[pl.ds(at, rows), :] = chunk[...]


def swap(array):
    unit = array.shape[1] // 2
    return jnp.concatenate([array[:, unit:], array[:, :unit]], axis=1)


def first_unit(array):
    return lax.broadcasted_iota(jnp.int32, array.shape, 1) < array.shape[1] // 2


def quarters(*arrays):
    size = arrays[0].shape[0] // 4
    return jnp.concatenate(
        [array[at * size : (at + 1) * size] for at, array in enumerate(arrays)], axis=0
    )


def spectrum(forward, top, bottom):
    both = dot(forward[...], jnp.concatenate([top, bottom], axis=1))
    length, lanes = both.shape[0] // 2, top.shape[1]
    real, imag = both[:length, lanes:], both[length:, lanes:]
    plus, minus = (real + imag) * HALF_TURN, (real - imag) * HALF_TURN
    return (
        both[:length, :lanes] + quarters(minus, -plus, -minus, plus),
        both[length:, :lanes] + quarters(plus, minus, -plus, -minus),
    )


def inverse(backward, real, imag):
    plus, minus = (real + imag) * HALF_TURN, (real - imag) * HALF_TURN
    real = jnp.concatenate([real, quarters(plus, -minus, -plus, minus)], axis=1)
    imag = jnp.concatenate([imag, quarters(-minus, -plus, minus, plus)], axis=1)
    return dot(backward[...], jnp.concatenate([real, imag], axis=0).astype(BF16))


def times_conj(real, imag, other_real, other_imag):
    return real * other_real + imag * other_imag, imag * other_real - real * other_imag


def halves(array):
    size, lanes = array.shape[0] // 2, array.shape[1] // 2
    return [
        (array[part * size : (part + 1) * size, :lanes], array[part * size : (part + 1) * size, lanes:])
        for part in range(2)
    ]


def first_tick(gain, forward, backward, *rest):
    *chunks, out, spectra, held = rest
    gather_positions(chunks, first_steps(len(chunks)), held)
    length, lanes = held.shape[0], gain.shape[1]
    parts = halves(held)
    real, imag = spectrum(forward, parts[0][0], parts[1][0])
    spectra[0], spectra[1] = real, imag
    both = inverse(backward, *times_conj(real, imag, swap(real), swap(imag))) * (1.0 / length)
    gradients = []
    for part, (first, second) in enumerate(parts):
        correlated = both[:, part * lanes : (part + 1) * lanes]
        kept = second.astype(F32)
        gradient = kept + swap(kept) * (correlated + gain[...] * first.astype(F32))
        gradients.append(jnp.where(lax.axis_index("section") == 0, kept, gradient))
    top, bottom = gradients
    out[...] = jnp.where(first_unit(top), swap(top), bottom).astype(BF16)


def mixed_spectra(scale, forward, spectra, *rest):
    *chunks, post, weight, other, lag_spec, held = rest
    gather_positions(chunks, second_steps(len(chunks)), held)
    parts = halves(held)
    real, imag = spectrum(forward, parts[0][0], parts[1][0])
    low = first_unit(real)
    other[0] = jnp.where(low, spectra[0], real)
    other[1] = jnp.where(low, spectra[1], imag)
    lag_real, lag_imag = times_conj(spectra[0], spectra[1], swap(real), swap(imag))
    lag_spec[0] = jnp.where(low, 0.0, lag_real)
    lag_spec[1] = jnp.where(low, 0.0, lag_imag)
    for part, (_, gates) in enumerate(parts):
        gates = gates.astype(F32)
        low = first_unit(gates)
        post[part] = jnp.where(low, gates, swap(gates))
        weight[part] = jnp.where(low, swap(gates), scale)


def second_tick(gain, forward, backward, received, post, weight, other, lag_spec, *rest):
    *outs, stage = rest
    count, rows, lanes = stage.shape
    length = count * rows
    carried = received[...].astype(F32)
    low = first_unit(carried)
    carried = [jnp.where(low, carried, swap(carried)), jnp.where(low, swap(carried), carried)]
    gated = [(post[part] * carried[part]).astype(BF16) for part in range(2)]
    real, imag = times_conj(*spectrum(forward, *gated), other[0], other[1])
    both = inverse(backward, real + lag_spec[0], imag + lag_spec[1]) * (1.0 / length)
    for part in range(2):
        skipped = jnp.where(low, gain[...] * gated[part].astype(F32), 0.0)
        result = weight[part] * (both[:, part * lanes : (part + 1) * lanes] + skipped)
        result = jnp.where(low, carried[part] + result, result).astype(BF16)
        for block in range(count // 2):
            stage[part * (count // 2) + block] = result[block * rows : (block + 1) * rows]
    for step, out in zip([OWN, *last_steps(count)], outs):
        out[...] = stage[place(step)]


def unpack_gradient(*rest):
    *chunks, grad, stage = rest
    count = stage.shape[0]
    unit = stage.shape[2] // 2
    for step, chunk in zip([OWN, *last_steps(count)], chunks):
        stage[place(step)] = chunk[...]
    grad[0] = jnp.concatenate([stage[block][:, :unit] for block in range(count)], axis=1)


def unpack_lags(*rest):
    *refs, stage, lag_stage = rest
    count = stage.shape[0]
    chunks, lags = refs[:count], refs[count:]
    unit = stage.shape[2] // 2
    chan_index = lax.axis_index("chan")
    for step, chunk in zip([OWN, *last_steps(count)], chunks):
        stage[place(step)] = chunk[...]
    lag_grad = jnp.concatenate([stage[block][:, unit:] for block in range(count)], axis=1)
    lag_stage[...] = lag_grad.astype(F32).T.astype(BF16)
    for step, lag in enumerate(lags):
        width = lag.shape[0]
        lag[...] = lag_stage[pl.ds(pl.multiple_of((chan_index ^ step) * width, width), width), :]


def add_up(*refs):
    *lags, out = refs
    out[...] = functools.reduce(jnp.add, [lag[...].astype(F32) for lag in lags])


def exchange_chan(chunks):
    size = lax.axis_size("chan")
    return [chunks[0]] + [
        lax.ppermute(chunks[step], "chan", [(i, i ^ step) for i in range(size)])
        for step in reversed(range(1, size))
    ]


def exchange_seq(chunks, steps):
    size = lax.axis_size("seq")
    places = [(section, seq) for section in range(lax.axis_size("section")) for seq in range(size)]
    return [chunks[0]] + [
        lax.ppermute(
            chunk,
            ("section", "seq"),
            [
                (section * size + seq, section * size + (seq ^ step[section % 2]))
                for section, seq in places
            ],
        )
        for chunk, step in zip(chunks[1:], steps)
    ]


def body(forward, backward, *args):
    saved_input, pre_gate, post_gate, grad_held, loss_grad, filters, skip_gain = args
    seq_count = lax.axis_size("seq")
    chan_count = lax.axis_size("chan")
    section_count = lax.axis_size("section")
    _, tick_count, rows, width = saved_input.shape
    length = rows * seq_count
    unit = width // seq_count
    forward, backward = jnp.asarray(forward), jnp.asarray(backward)
    scale = 1.0 / math.sqrt(length * chan_count * tick_count)
    struct = jax.ShapeDtypeStruct
    chunk = struct((rows, 4 * unit), BF16)
    stage = struct((seq_count, rows, 4 * unit), BF16)
    held_rows = struct((length, 4 * unit), BF16)
    two_spectra = struct((2, length, 2 * unit), F32)
    two_parts = struct((2, length // 2, 2 * unit), F32)

    first = call(
        pack_first,
        [chunk] * seq_count,
        [stage, struct((4, rows, width), BF16), struct((rows, width), F32)],
        [pltpu.HBM] * 5,
        5,
    )(post_gate, grad_held, loss_grad, pre_gate, filters)
    *second, gain, forward, backward = call(
        pack_second,
        [chunk] * seq_count
        + [
            struct((1, 2 * unit), F32),
            struct(forward.shape, BF16),
            struct(backward.shape, BF16),
        ],
        [stage, struct((5, rows, width), BF16), struct((1, width), F32)],
        [pl.ANY] + [pltpu.HBM] * 6,
        8,
    )(first[0], saved_input, pre_gate, post_gate, skip_gain, forward, backward)
    first = exchange_seq(first, first_steps(seq_count))
    second = exchange_seq(second, second_steps(seq_count))

    gradient, spectra = call(
        first_tick,
        [struct((length // 2, 2 * unit), BF16), two_spectra],
        [held_rows],
    )(gain, forward, backward, *first)
    ring = [(i, (i - 1) % section_count) for i in range(section_count)]
    received = lax.ppermute(gradient, "section", ring)

    prepared = call(
        functools.partial(mixed_spectra, scale),
        [two_parts, two_parts, two_spectra, two_spectra],
        [held_rows],
    )(forward, spectra, *second)

    sorted_chunks = struct((seq_count, rows, 2 * unit), BF16)
    result = call(
        second_tick,
        [struct((rows, 2 * unit), BF16)] * seq_count,
        [sorted_chunks],
    )(gain, forward, backward, received, *prepared)
    result = exchange_seq(result, last_steps(seq_count))

    lag_width = width // chan_count
    lags = call(
        unpack_lags,
        [struct((lag_width, rows), BF16)] * chan_count,
        [sorted_chunks, struct((width, rows), BF16)],
    )(*result)
    lags = exchange_chan(lags)
    (grad_out,) = call(unpack_gradient, [struct((1, rows, width), BF16)], [sorted_chunks])(*result)
    (lag_grad,) = call(add_up, [struct((lag_width, rows), F32)])(*lags)
    return grad_out, lag_grad.T[None]


def solution(mesh):
    placed = (
        P("section", None, "seq", "chan"),
        P("section", None, "seq", "chan"),
        P("section", None, "seq", "chan"),
        P("section", "seq", "chan"),
        P("seq", "chan"),
        P("section", "seq", None),
        P("section", None),
    )

    def program(*args):
        return jax.shard_map(
            functools.partial(body, *transform_tables(args[0].shape[2])),
            mesh=mesh,
            in_specs=placed,
            out_specs=(P("section", "seq", "chan"), P("section", "seq", "chan")),
            check_vma=False,
        )(*args)

    return program
```

```python
import functools
import math

import jax
import jax.numpy as jnp
import ml_dtypes
import numpy as np
from jax import lax
from jax.experimental import pallas as pl
from jax.experimental.pallas import tpu as pltpu
from jax.sharding import PartitionSpec as P

BF16 = jnp.bfloat16
F32 = jnp.float32
HALF_TURN = math.sqrt(0.5)
OWN = (0, 0)


def both(steps):
    return [(step, step) for step in steps]


def first_steps(size):
    return both([*range(2, size), 1])


def second_steps(size):
    near = list(range(1, size))
    return list(zip(near, [*near[1::-1], *near[2:]]))


def last_steps(size):
    return both([size - 1, *range(1, size - 1)])


def transform_tables(length):
    freq = np.concatenate([np.arange(rest, length, 4, dtype=np.int64) for rest in range(4)])
    position = np.arange(length // 2, dtype=np.int64)
    angles = math.pi / (2 * length) * ((2 * freq[:, None] + 1) * position[None, :] % (4 * length))
    table = np.concatenate([np.cos(angles), np.sin(angles)], axis=0).astype(ml_dtypes.bfloat16)
    return table, np.ascontiguousarray(table.T)


def size_of(shapes):
    total = 0
    for shape in shapes:
        lanes = -(-shape.shape[-1] // 128) * 128
        total += math.prod(shape.shape[:-1]) * lanes * jnp.dtype(shape.dtype).itemsize
    return total


def call(kernel, out_shape, scratch=(), spaces=None, copies=0):
    def run(*arrays):
        held = size_of([*arrays, *out_shape, *scratch])
        if spaces:
            arrays = [
                pltpu.with_memory_space_constraint(array, space) if space == pltpu.HBM else array
                for array, space in zip(arrays, spaces)
            ]
        scratch_shapes = [pltpu.VMEM(shape.shape, shape.dtype) for shape in scratch]
        if copies:
            scratch_shapes.append(pltpu.SemaphoreType.DMA((copies,)))
        return pl.pallas_call(
            kernel,
            out_shape=out_shape,
            in_specs=[
                pl.BlockSpec(memory_space=space)
                for space in spaces or [pltpu.VMEM] * len(arrays)
            ],
            scratch_shapes=scratch_shapes,
            compiler_params=pltpu.CompilerParams(vmem_limit_bytes=2 * held + (4 << 20)),
        )(*arrays)

    return run


def fetch(sources, places, semaphores):
    copies = [
        pltpu.make_async_copy(source, place, semaphores.at[at])
        for at, (source, place) in enumerate(zip(sources, places))
    ]
    for copy in copies:
        copy.start()
    return copies


def wait(copies):
    for copy in copies:
        copy.wait()


def dot(left, right):
    return jnp.dot(left, right, preferred_element_type=F32)


def place(step):
    even, odd = step
    return lax.axis_index("seq") ^ jnp.where(lax.axis_index("section") % 2 == 0, even, odd)


def pack(arrays, stage, outs, steps):
    count = len(outs)
    unit = arrays[0].shape[1] // count
    for block in range(count):
        lanes = slice(block * unit, (block + 1) * unit)
        stage[block] = jnp.concatenate([array[:, lanes] for array in arrays], axis=1)
    for step, out in zip([OWN, *steps], outs):
        out[...] = stage[place(step)]


def pack_first(post, held, loss, pre, filters, *rest):
    *outs, stage, gates, lags, semaphores = rest
    sources = [post.at[0, 0], held.at[0], loss, pre.at[0, 0], filters.at[0]]
    wait(fetch(sources, [gates.at[at] for at in range(4)] + [lags], semaphores))
    gated = (gates[0].astype(F32) * gates[1].astype(F32)).astype(BF16)
    kept = jnp.where(lax.axis_index("section") == 0, gates[2], gates[1])
    pack([lags[...].astype(BF16), gated, gates[3], kept], stage, outs, first_steps(len(outs)))


def pack_second(after, saved, pre, post, gains, forward, backward, *rest):
    del after
    *outs, gain, forward_out, backward_out, stage, gates, all_gains, semaphores = rest
    sources = [saved.at[0, 0], saved.at[0, 1], pre.at[0, 0], pre.at[0, 1], post.at[0, 1]]
    places = [gates.at[at] for at in range(5)]
    copies = fetch(
        [*sources, gains, forward, backward],
        [*places, all_gains, forward_out, backward_out],
        semaphores,
    )
    wait(copies[:6])
    mixed = (gates[0:2].astype(F32) * gates[2:4].astype(F32)).astype(BF16)
    pack([mixed[0], mixed[1], gates[4], gates[3]], stage, outs, second_steps(len(outs)))
    unit = gain.shape[1] // 2
    for block in range(len(outs)):

        @pl.when(lax.axis_index("seq") == block)
        def _():
            own = all_gains[:, block * unit : (block + 1) * unit]
            gain[...] = jnp.concatenate([own, own], axis=1)

    wait(copies[6:])


def gather_positions(chunks, steps, held):
    rows = chunks[0].shape[0]
    for step, chunk in zip([OWN, *steps], chunks):
        at = pl.multiple_of(place(step) * rows, rows)
        held[pl.ds(at, rows), :] = chunk[...]


def swap(array):
    unit = array.shape[1] // 2
    return jnp.concatenate([array[:, unit:], array[:, :unit]], axis=1)


def first_unit(array):
    return lax.broadcasted_iota(jnp.int32, array.shape, 1) < array.shape[1] // 2


def quarters(*arrays):
    size = arrays[0].shape[0] // 4
    return jnp.concatenate(
        [array[at * size : (at + 1) * size] for at, array in enumerate(arrays)], axis=0
    )


def spectrum(forward, top, bottom):
    both = dot(forward[...], jnp.concatenate([top, bottom], axis=1))
    length, lanes = both.shape[0] // 2, top.shape[1]
    real, imag = both[:length, lanes:], both[length:, lanes:]
    plus, minus = (real + imag) * HALF_TURN, (real - imag) * HALF_TURN
    return (
        both[:length, :lanes] + quarters(minus, -plus, -minus, plus),
        both[length:, :lanes] + quarters(plus, minus, -plus, -minus),
    )


def inverse(backward, real, imag):
    length, lanes = real.shape
    plus, minus = real + imag, real - imag
    real = jnp.concatenate([real, quarters(plus, -minus, -plus, minus)], axis=1)
    imag = jnp.concatenate([imag, quarters(-minus, -plus, minus, plus)], axis=1)
    sums = dot(backward[...], jnp.concatenate([real, imag], axis=0).astype(BF16))
    return sums[:, :lanes] * (1.0 / length), sums[:, lanes:] * (HALF_TURN / length)


def times_conj(real, imag, other_real, other_imag):
    return real * other_real + imag * other_imag, imag * other_real - real * other_imag


def halves(array):
    size, lanes = array.shape[0] // 2, array.shape[1] // 2
    return [
        (array[part * size : (part + 1) * size, :lanes], array[part * size : (part + 1) * size, lanes:])
        for part in range(2)
    ]


def first_tick(gain, forward, backward, *rest):
    *chunks, out, spectra, held = rest
    gather_positions(chunks, first_steps(len(chunks)), held)
    parts = halves(held)
    real, imag = spectrum(forward, parts[0][0], parts[1][0])
    spectra[0], spectra[1] = real, imag
    convolved = inverse(backward, *times_conj(real, imag, swap(real), swap(imag)))
    gradients = []
    for part, (first, second) in enumerate(parts):
        kept = second.astype(F32)
        gradient = kept + swap(kept) * (convolved[part] + gain[...] * first.astype(F32))
        gradients.append(jnp.where(lax.axis_index("section") == 0, kept, gradient))
    top, bottom = gradients
    out[...] = jnp.where(first_unit(top), swap(top), bottom).astype(BF16)


def mixed_spectra(scale, forward, spectra, *rest):
    *chunks, post, weight, other, lag_spec, held = rest
    gather_positions(chunks, second_steps(len(chunks)), held)
    parts = halves(held)
    real, imag = spectrum(forward, parts[0][0], parts[1][0])
    low = first_unit(real)
    other[0] = jnp.where(low, spectra[0], real)
    other[1] = jnp.where(low, spectra[1], imag)
    lag_real, lag_imag = times_conj(spectra[0], spectra[1], swap(real), swap(imag))
    lag_spec[0] = jnp.where(low, 0.0, lag_real)
    lag_spec[1] = jnp.where(low, 0.0, lag_imag)
    for part, (_, gates) in enumerate(parts):
        gates = gates.astype(F32)
        low = first_unit(gates)
        post[part] = jnp.where(low, gates, swap(gates))
        weight[part] = jnp.where(low, swap(gates), scale)


def second_tick(gain, forward, backward, received, post, weight, other, lag_spec, *rest):
    *outs, stage = rest
    count, rows, _ = stage.shape
    carried = received[...].astype(F32)
    low = first_unit(carried)
    carried = [jnp.where(low, carried, swap(carried)), jnp.where(low, swap(carried), carried)]
    gated = [(post[part] * carried[part]).astype(BF16) for part in range(2)]
    real, imag = times_conj(*spectrum(forward, *gated), other[0], other[1])
    convolved = inverse(backward, real + lag_spec[0], imag + lag_spec[1])
    for part in range(2):
        skipped = jnp.where(low, gain[...] * gated[part].astype(F32), 0.0)
        result = weight[part] * (convolved[part] + skipped)
        result = jnp.where(low, carried[part] + result, result).astype(BF16)
        for block in range(count // 2):
            stage[part * (count // 2) + block] = result[block * rows : (block + 1) * rows]
    for step, out in zip([OWN, *last_steps(count)], outs):
        out[...] = stage[place(step)]


def unpack_gradient(*rest):
    *chunks, grad, stage = rest
    count = stage.shape[0]
    unit = stage.shape[2] // 2
    for step, chunk in zip([OWN, *last_steps(count)], chunks):
        stage[place(step)] = chunk[...]
    grad[0] = jnp.concatenate([stage[block][:, :unit] for block in range(count)], axis=1)


def unpack_lags(*rest):
    *refs, stage, lag_stage = rest
    count = stage.shape[0]
    chunks, lags = refs[:count], refs[count:]
    unit = stage.shape[2] // 2
    chan_index = lax.axis_index("chan")
    for step, chunk in zip([OWN, *last_steps(count)], chunks):
        stage[place(step)] = chunk[...]
    lag_grad = jnp.concatenate([stage[block][:, unit:] for block in range(count)], axis=1)
    lag_stage[...] = lag_grad.astype(F32).T.astype(BF16)
    for step, lag in enumerate(lags):
        width = lag.shape[0]
        lag[...] = lag_stage[pl.ds(pl.multiple_of((chan_index ^ step) * width, width), width), :]


def add_up(*refs):
    *lags, out = refs
    out[...] = functools.reduce(jnp.add, [lag[...].astype(F32) for lag in lags])


def exchange_chan(chunks):
    size = lax.axis_size("chan")
    return [chunks[0]] + [
        lax.ppermute(chunks[step], "chan", [(i, i ^ step) for i in range(size)])
        for step in reversed(range(1, size))
    ]


def exchange_seq(chunks, steps):
    size = lax.axis_size("seq")
    places = [(section, seq) for section in range(lax.axis_size("section")) for seq in range(size)]
    return [chunks[0]] + [
        lax.ppermute(
            chunk,
            ("section", "seq"),
            [
                (section * size + seq, section * size + (seq ^ step[section % 2]))
                for section, seq in places
            ],
        )
        for chunk, step in zip(chunks[1:], steps)
    ]


def body(forward, backward, *args):
    saved_input, pre_gate, post_gate, grad_held, loss_grad, filters, skip_gain = args
    seq_count = lax.axis_size("seq")
    chan_count = lax.axis_size("chan")
    section_count = lax.axis_size("section")
    _, tick_count, rows, width = saved_input.shape
    length = rows * seq_count
    unit = width // seq_count
    forward, backward = jnp.asarray(forward), jnp.asarray(backward)
    scale = 1.0 / math.sqrt(length * chan_count * tick_count)
    struct = jax.ShapeDtypeStruct
    chunk = struct((rows, 4 * unit), BF16)
    stage = struct((seq_count, rows, 4 * unit), BF16)
    held_rows = struct((length, 4 * unit), BF16)
    two_spectra = struct((2, length, 2 * unit), F32)
    two_parts = struct((2, length // 2, 2 * unit), F32)

    first = call(
        pack_first,
        [chunk] * seq_count,
        [stage, struct((4, rows, width), BF16), struct((rows, width), F32)],
        [pltpu.HBM] * 5,
        5,
    )(post_gate, grad_held, loss_grad, pre_gate, filters)
    *second, gain, forward, backward = call(
        pack_second,
        [chunk] * seq_count
        + [
            struct((1, 2 * unit), F32),
            struct(forward.shape, BF16),
            struct(backward.shape, BF16),
        ],
        [stage, struct((5, rows, width), BF16), struct((1, width), F32)],
        [pl.ANY] + [pltpu.HBM] * 6,
        8,
    )(first[0], saved_input, pre_gate, post_gate, skip_gain, forward, backward)
    first = exchange_seq(first, first_steps(seq_count))
    second = exchange_seq(second, second_steps(seq_count))

    gradient, spectra = call(
        first_tick,
        [struct((length // 2, 2 * unit), BF16), two_spectra],
        [held_rows],
    )(gain, forward, backward, *first)
    ring = [(i, (i - 1) % section_count) for i in range(section_count)]
    received = lax.ppermute(gradient, "section", ring)

    prepared = call(
        functools.partial(mixed_spectra, scale),
        [two_parts, two_parts, two_spectra, two_spectra],
        [held_rows],
    )(forward, spectra, *second)

    sorted_chunks = struct((seq_count, rows, 2 * unit), BF16)
    result = call(
        second_tick,
        [struct((rows, 2 * unit), BF16)] * seq_count,
        [sorted_chunks],
    )(gain, forward, backward, received, *prepared)
    result = exchange_seq(result, last_steps(seq_count))

    lag_width = width // chan_count
    lags = call(
        unpack_lags,
        [struct((lag_width, rows), BF16)] * chan_count,
        [sorted_chunks, struct((width, rows), BF16)],
    )(*result)
    lags = exchange_chan(lags)
    (grad_out,) = call(unpack_gradient, [struct((1, rows, width), BF16)], [sorted_chunks])(*result)
    (lag_grad,) = call(add_up, [struct((lag_width, rows), F32)])(*lags)
    return grad_out, lag_grad.T[None]


def solution(mesh):
    placed = (
        P("section", None, "seq", "chan"),
        P("section", None, "seq", "chan"),
        P("section", None, "seq", "chan"),
        P("section", "seq", "chan"),
        P("seq", "chan"),
        P("section", "seq", None),
        P("section", None),
    )

    def program(*args):
        return jax.shard_map(
            functools.partial(body, *transform_tables(args[0].shape[2])),
            mesh=mesh,
            in_specs=placed,
            out_specs=(P("section", "seq", "chan"), P("section", "seq", "chan")),
            check_vma=False,
        )(*args)

    return program
```

```python
import functools
import math

import jax
import jax.numpy as jnp
import ml_dtypes
import numpy as np
from jax import lax
from jax.experimental import pallas as pl
from jax.experimental.pallas import tpu as pltpu
from jax.sharding import PartitionSpec as P

BF16 = jnp.bfloat16
F32 = jnp.float32
HALF_TURN = math.sqrt(0.5)
OWN = (0, 0)


def both(steps):
    return [(step, step) for step in steps]


def first_steps(size):
    return both([*range(2, size), 1])


def second_steps(size):
    near = list(range(1, size))
    return list(zip(near, [*near[1::-1], *near[2:]]))


def last_steps(size):
    return both([size - 1, *range(1, size - 1)])


def transform_tables(length):
    freq = np.concatenate([np.arange(rest, length, 4, dtype=np.int64) for rest in range(4)])
    position = np.arange(length // 2, dtype=np.int64)
    angles = math.pi / (2 * length) * ((2 * freq[:, None] + 1) * position[None, :] % (4 * length))
    table = np.concatenate([np.cos(angles), np.sin(angles)], axis=0).astype(ml_dtypes.bfloat16)
    return table, np.ascontiguousarray(table.T)


def size_of(shapes):
    total = 0
    for shape in shapes:
        lanes = -(-shape.shape[-1] // 128) * 128
        total += math.prod(shape.shape[:-1]) * lanes * jnp.dtype(shape.dtype).itemsize
    return total


def call(kernel, out_shape, scratch=(), spaces=None, copies=0):
    def run(*arrays):
        held = size_of([*arrays, *out_shape, *scratch])
        if spaces:
            arrays = [
                pltpu.with_memory_space_constraint(array, space) if space == pltpu.HBM else array
                for array, space in zip(arrays, spaces)
            ]
        scratch_shapes = [pltpu.VMEM(shape.shape, shape.dtype) for shape in scratch]
        if copies:
            scratch_shapes.append(pltpu.SemaphoreType.DMA((copies,)))
        return pl.pallas_call(
            kernel,
            out_shape=out_shape,
            in_specs=[
                pl.BlockSpec(memory_space=space)
                for space in spaces or [pltpu.VMEM] * len(arrays)
            ],
            scratch_shapes=scratch_shapes,
            compiler_params=pltpu.CompilerParams(vmem_limit_bytes=2 * held + (4 << 20)),
        )(*arrays)

    return run


def fetch(sources, places, semaphores):
    copies = [
        pltpu.make_async_copy(source, place, semaphores.at[at])
        for at, (source, place) in enumerate(zip(sources, places))
    ]
    for copy in copies:
        copy.start()
    return copies


def wait(copies):
    for copy in copies:
        copy.wait()


def dot(left, right):
    return jnp.dot(left, right, preferred_element_type=F32)


def place(step):
    even, odd = step
    return lax.axis_index("seq") ^ jnp.where(lax.axis_index("section") % 2 == 0, even, odd)


def pack(arrays, stage, outs, steps):
    count = len(outs)
    unit = arrays[0].shape[1] // count
    for block in range(count):
        lanes = slice(block * unit, (block + 1) * unit)
        stage[block] = jnp.concatenate([array[:, lanes] for array in arrays], axis=1)
    for step, out in zip([OWN, *steps], outs):
        out[...] = stage[place(step)]


def pack_first(post, held, loss, pre, filters, *rest):
    *outs, stage, gates, lags, semaphores = rest
    sources = [post.at[0, 0], held.at[0], loss, pre.at[0, 0], filters.at[0]]
    wait(fetch(sources, [gates.at[at] for at in range(4)] + [lags], semaphores))
    gated = (gates[0].astype(F32) * gates[1].astype(F32)).astype(BF16)
    kept = jnp.where(lax.axis_index("section") == 0, gates[2], gates[1])
    pack([lags[...].astype(BF16), gated, gates[3], kept], stage, outs, first_steps(len(outs)))


def pack_second(after, saved, pre, post, gains, forward, backward, *rest):
    del after
    *outs, gain, forward_out, backward_out, stage, gates, all_gains, semaphores = rest
    sources = [saved.at[0, 0], saved.at[0, 1], pre.at[0, 0], pre.at[0, 1], post.at[0, 1]]
    places = [gates.at[at] for at in range(5)]
    copies = fetch(
        [*sources, gains, forward, backward],
        [*places, all_gains, forward_out, backward_out],
        semaphores,
    )
    wait(copies[:6])
    mixed = (gates[0:2].astype(F32) * gates[2:4].astype(F32)).astype(BF16)
    pack([mixed[0], mixed[1], gates[4], gates[3]], stage, outs, second_steps(len(outs)))
    unit = gain.shape[1] // 2
    for block in range(len(outs)):

        @pl.when(lax.axis_index("seq") == block)
        def _():
            own = all_gains[:, block * unit : (block + 1) * unit]
            gain[...] = jnp.concatenate([own, own], axis=1)

    wait(copies[6:])


def gather_positions(chunks, steps, held):
    rows = chunks[0].shape[0]
    for step, chunk in zip([OWN, *steps], chunks):
        at = pl.multiple_of(place(step) * rows, rows)
        held[pl.ds(at, rows), :] = chunk[...]


def swap(array):
    unit = array.shape[1] // 2
    return jnp.concatenate([array[:, unit:], array[:, :unit]], axis=1)


def first_unit(array):
    return lax.broadcasted_iota(jnp.int32, array.shape, 1) < array.shape[1] // 2


def quarters(*arrays):
    size = arrays[0].shape[0] // 4
    return jnp.concatenate(
        [array[at * size : (at + 1) * size] for at, array in enumerate(arrays)], axis=0
    )


def spectrum(forward, top, bottom):
    both = dot(forward[...], jnp.concatenate([top, bottom], axis=1))
    length, lanes = both.shape[0] // 2, top.shape[1]
    real, imag = both[:length, lanes:], both[length:, lanes:]
    plus, minus = (real + imag) * HALF_TURN, (real - imag) * HALF_TURN
    return (
        both[:length, :lanes] + quarters(minus, -plus, -minus, plus),
        both[length:, :lanes] + quarters(plus, minus, -plus, -minus),
    )


def inverse(backward, real, imag):
    length, lanes = real.shape
    plus, minus = real + imag, real - imag
    real = jnp.concatenate([real, quarters(plus, -minus, -plus, minus)], axis=1)
    imag = jnp.concatenate([imag, quarters(-minus, -plus, minus, plus)], axis=1)
    sums = dot(backward[...], jnp.concatenate([real, imag], axis=0).astype(BF16))
    return sums[:, :lanes] * (1.0 / length), sums[:, lanes:] * (HALF_TURN / length)


def times_conj(real, imag, other_real, other_imag):
    return real * other_real + imag * other_imag, imag * other_real - real * other_imag


def halves(array):
    size, lanes = array.shape[0] // 2, array.shape[1] // 2
    return [
        (array[part * size : (part + 1) * size, :lanes], array[part * size : (part + 1) * size, lanes:])
        for part in range(2)
    ]


def first_tick(gain, forward, backward, *rest):
    *chunks, out, spectra, held = rest
    gather_positions(chunks, first_steps(len(chunks)), held)
    parts = halves(held)
    real, imag = spectrum(forward, parts[0][0], parts[1][0])
    spectra[0], spectra[1] = real, imag
    convolved = inverse(backward, *times_conj(real, imag, swap(real), swap(imag)))
    gradients = []
    for part, (first, second) in enumerate(parts):
        kept = second.astype(F32)
        gradient = kept + swap(kept) * (convolved[part] + gain[...] * first.astype(F32))
        gradients.append(jnp.where(lax.axis_index("section") == 0, kept, gradient))
    top, bottom = gradients
    out[...] = jnp.where(first_unit(top), swap(top), bottom).astype(BF16)


def mixed_spectra(scale, forward, spectra, *rest):
    *chunks, post, weight, other, lag_spec, held = rest
    gather_positions(chunks, second_steps(len(chunks)), held)
    parts = halves(held)
    real, imag = spectrum(forward, parts[0][0], parts[1][0])
    low = first_unit(real)
    other[0] = jnp.where(low, spectra[0], real)
    other[1] = jnp.where(low, spectra[1], imag)
    lag_real, lag_imag = times_conj(spectra[0], spectra[1], swap(real), swap(imag))
    lag_spec[0] = jnp.where(low, 0.0, lag_real)
    lag_spec[1] = jnp.where(low, 0.0, lag_imag)
    for part, (_, gates) in enumerate(parts):
        gates = gates.astype(F32)
        low = first_unit(gates)
        post[part] = jnp.where(low, gates, swap(gates))
        weight[part] = jnp.where(low, swap(gates), scale)


def second_tick(gain, forward, backward, received, post, weight, other, lag_spec, *rest):
    *outs, stage = rest
    count, rows, _ = stage.shape
    carried = received[...].astype(F32)
    low = first_unit(carried)
    carried = [jnp.where(low, carried, swap(carried)), jnp.where(low, swap(carried), carried)]
    gated = [(post[part] * carried[part]).astype(BF16) for part in range(2)]
    real, imag = times_conj(*spectrum(forward, *gated), other[0], other[1])
    convolved = inverse(backward, real + lag_spec[0], imag + lag_spec[1])
    for part in range(2):
        skipped = jnp.where(low, gain[...] * gated[part].astype(F32), 0.0)
        result = weight[part] * (convolved[part] + skipped)
        result = jnp.where(low, carried[part] + result, result).astype(BF16)
        for block in range(count // 2):
            stage[part * (count // 2) + block] = result[block * rows : (block + 1) * rows]
    for step, out in zip([OWN, *last_steps(count)], outs):
        out[...] = stage[place(step)]


def unpack_gradient(*rest):
    *chunks, grad, stage = rest
    count = stage.shape[0]
    unit = stage.shape[2] // 2
    for step, chunk in zip([OWN, *last_steps(count)], chunks):
        stage[place(step)] = chunk[...]
    grad[0] = jnp.concatenate([stage[block][:, :unit] for block in range(count)], axis=1)


def unpack_lags(*rest):
    *refs, stage, lag_stage = rest
    count = stage.shape[0]
    chunks, lags = refs[:count], refs[count:]
    unit = stage.shape[2] // 2
    chan_index = lax.axis_index("chan")
    for step, chunk in zip([OWN, *last_steps(count)], chunks):
        stage[place(step)] = chunk[...]
    lag_grad = jnp.concatenate([stage[block][:, unit:] for block in range(count)], axis=1)
    lag_stage[...] = lag_grad.T
    for step, lag in enumerate(lags):
        width = lag.shape[0]
        lag[...] = lag_stage[pl.ds(pl.multiple_of((chan_index ^ step) * width, width), width), :]


def add_up(*refs):
    *lags, out = refs
    out[...] = functools.reduce(jnp.add, [lag[...].astype(F32) for lag in lags])


def exchange_chan(chunks):
    size = lax.axis_size("chan")
    return [chunks[0]] + [
        lax.ppermute(chunks[step], "chan", [(i, i ^ step) for i in range(size)])
        for step in reversed(range(1, size))
    ]


def exchange_seq(chunks, steps):
    size = lax.axis_size("seq")
    places = [(section, seq) for section in range(lax.axis_size("section")) for seq in range(size)]
    return [chunks[0]] + [
        lax.ppermute(
            chunk,
            ("section", "seq"),
            [
                (section * size + seq, section * size + (seq ^ step[section % 2]))
                for section, seq in places
            ],
        )
        for chunk, step in zip(chunks[1:], steps)
    ]


def body(forward, backward, *args):
    saved_input, pre_gate, post_gate, grad_held, loss_grad, filters, skip_gain = args
    seq_count = lax.axis_size("seq")
    chan_count = lax.axis_size("chan")
    section_count = lax.axis_size("section")
    _, tick_count, rows, width = saved_input.shape
    length = rows * seq_count
    unit = width // seq_count
    forward, backward = jnp.asarray(forward), jnp.asarray(backward)
    scale = 1.0 / math.sqrt(length * chan_count * tick_count)
    struct = jax.ShapeDtypeStruct
    chunk = struct((rows, 4 * unit), BF16)
    stage = struct((seq_count, rows, 4 * unit), BF16)
    held_rows = struct((length, 4 * unit), BF16)
    two_spectra = struct((2, length, 2 * unit), F32)
    two_parts = struct((2, length // 2, 2 * unit), F32)

    first = call(
        pack_first,
        [chunk] * seq_count,
        [stage, struct((4, rows, width), BF16), struct((rows, width), F32)],
        [pltpu.HBM] * 5,
        5,
    )(post_gate, grad_held, loss_grad, pre_gate, filters)
    *second, gain, forward, backward = call(
        pack_second,
        [chunk] * seq_count
        + [
            struct((1, 2 * unit), F32),
            struct(forward.shape, BF16),
            struct(backward.shape, BF16),
        ],
        [stage, struct((5, rows, width), BF16), struct((1, width), F32)],
        [pl.ANY] + [pltpu.HBM] * 6,
        8,
    )(first[0], saved_input, pre_gate, post_gate, skip_gain, forward, backward)
    first = exchange_seq(first, first_steps(seq_count))
    second = exchange_seq(second, second_steps(seq_count))

    gradient, spectra = call(
        first_tick,
        [struct((length // 2, 2 * unit), BF16), two_spectra],
        [held_rows],
    )(gain, forward, backward, *first)
    ring = [(i, (i - 1) % section_count) for i in range(section_count)]
    received = lax.ppermute(gradient, "section", ring)

    prepared = call(
        functools.partial(mixed_spectra, scale),
        [two_parts, two_parts, two_spectra, two_spectra],
        [held_rows],
    )(forward, spectra, *second)

    sorted_chunks = struct((seq_count, rows, 2 * unit), BF16)
    result = call(
        second_tick,
        [struct((rows, 2 * unit), BF16)] * seq_count,
        [sorted_chunks],
    )(gain, forward, backward, received, *prepared)
    result = exchange_seq(result, last_steps(seq_count))

    lag_width = width // chan_count
    lags = call(
        unpack_lags,
        [struct((lag_width, rows), BF16)] * chan_count,
        [sorted_chunks, struct((width, rows), BF16)],
    )(*result)
    lags = exchange_chan(lags)
    (grad_out,) = call(unpack_gradient, [struct((1, rows, width), BF16)], [sorted_chunks])(*result)
    (lag_grad,) = call(add_up, [struct((lag_width, rows), F32)])(*lags)
    return grad_out, lag_grad.T[None]


def solution(mesh):
    placed = (
        P("section", None, "seq", "chan"),
        P("section", None, "seq", "chan"),
        P("section", None, "seq", "chan"),
        P("section", "seq", "chan"),
        P("seq", "chan"),
        P("section", "seq", None),
        P("section", None),
    )

    def program(*args):
        return jax.shard_map(
            functools.partial(body, *transform_tables(args[0].shape[2])),
            mesh=mesh,
            in_specs=placed,
            out_specs=(P("section", "seq", "chan"), P("section", "seq", "chan")),
            check_vma=False,
        )(*args)

    return program
```

```python
import functools
import math

import jax
import jax.numpy as jnp
import ml_dtypes
import numpy as np
from jax import lax
from jax.experimental import pallas as pl
from jax.experimental.pallas import tpu as pltpu
from jax.sharding import PartitionSpec as P

BF16 = jnp.bfloat16
F32 = jnp.float32
HALF_TURN = math.sqrt(0.5)
OWN = (0, 0)


def both(steps):
    return [(step, step) for step in steps]


def first_steps(size):
    return both([*range(2, size), 1])


def second_steps(size):
    near = list(range(1, size))
    return list(zip(near, [*near[1::-1], *near[2:]]))


def last_steps(size):
    return both([size - 1, *range(1, size - 1)])


def transform_tables(length):
    freq = np.concatenate([np.arange(rest, length, 4, dtype=np.int64) for rest in range(4)])
    position = np.arange(length // 2, dtype=np.int64)
    angles = math.pi / (2 * length) * ((2 * freq[:, None] + 1) * position[None, :] % (4 * length))
    table = np.concatenate([np.cos(angles), np.sin(angles)], axis=0).astype(ml_dtypes.bfloat16)
    return table, np.ascontiguousarray(table.T)


def size_of(shapes):
    total = 0
    for shape in shapes:
        lanes = -(-shape.shape[-1] // 128) * 128
        total += math.prod(shape.shape[:-1]) * lanes * jnp.dtype(shape.dtype).itemsize
    return total


def call(kernel, out_shape, scratch=(), spaces=None, copies=0):
    def run(*arrays):
        held = size_of([*arrays, *out_shape, *scratch])
        if spaces:
            arrays = [
                pltpu.with_memory_space_constraint(array, space) if space == pltpu.HBM else array
                for array, space in zip(arrays, spaces)
            ]
        scratch_shapes = [pltpu.VMEM(shape.shape, shape.dtype) for shape in scratch]
        if copies:
            scratch_shapes.append(pltpu.SemaphoreType.DMA((copies,)))
        return pl.pallas_call(
            kernel,
            out_shape=out_shape,
            in_specs=[
                pl.BlockSpec(memory_space=space)
                for space in spaces or [pltpu.VMEM] * len(arrays)
            ],
            scratch_shapes=scratch_shapes,
            compiler_params=pltpu.CompilerParams(vmem_limit_bytes=2 * held + (4 << 20)),
        )(*arrays)

    return run


def fetch(sources, places, semaphores):
    copies = [
        pltpu.make_async_copy(source, place, semaphores.at[at])
        for at, (source, place) in enumerate(zip(sources, places))
    ]
    for copy in copies:
        copy.start()
    return copies


def wait(copies):
    for copy in copies:
        copy.wait()


def dot(left, right):
    return jnp.dot(left, right, preferred_element_type=F32)


def place(step):
    even, odd = step
    return lax.axis_index("seq") ^ jnp.where(lax.axis_index("section") % 2 == 0, even, odd)


def pack(arrays, stage, outs, steps):
    count = len(outs)
    unit = arrays[0].shape[1] // count
    for block in range(count):
        lanes = slice(block * unit, (block + 1) * unit)
        stage[block] = jnp.concatenate([array[:, lanes] for array in arrays], axis=1)
    for step, out in zip([OWN, *steps], outs):
        out[...] = stage[place(step)]


def pack_first(post, held, loss, pre, filters, *rest):
    *outs, stage, gates, lags, semaphores = rest
    sources = [post.at[0, 0], held.at[0], loss, pre.at[0, 0], filters.at[0]]
    wait(fetch(sources, [gates.at[at] for at in range(4)] + [lags], semaphores))
    gated = gates[0] * gates[1]
    kept = jnp.where(lax.axis_index("section") == 0, gates[2], gates[1])
    pack([lags[...].astype(BF16), gated, gates[3], kept], stage, outs, first_steps(len(outs)))


def pack_second(after, saved, pre, post, gains, forward, backward, *rest):
    del after
    *outs, gain, forward_out, backward_out, stage, gates, all_gains, semaphores = rest
    sources = [saved.at[0, 0], saved.at[0, 1], pre.at[0, 0], pre.at[0, 1], post.at[0, 1]]
    places = [gates.at[at] for at in range(5)]
    copies = fetch(
        [*sources, gains, forward, backward],
        [*places, all_gains, forward_out, backward_out],
        semaphores,
    )
    wait(copies[:6])
    mixed = gates[0:2] * gates[2:4]
    pack([mixed[0], mixed[1], gates[4], gates[3]], stage, outs, second_steps(len(outs)))
    unit = gain.shape[1] // 2
    for block in range(len(outs)):

        @pl.when(lax.axis_index("seq") == block)
        def _():
            own = all_gains[:, block * unit : (block + 1) * unit]
            gain[...] = jnp.concatenate([own, own], axis=1)

    wait(copies[6:])


def gather_positions(chunks, steps, held):
    rows = chunks[0].shape[0]
    for step, chunk in zip([OWN, *steps], chunks):
        at = pl.multiple_of(place(step) * rows, rows)
        held[pl.ds(at, rows), :] = chunk[...]


def swap(array):
    unit = array.shape[1] // 2
    return jnp.concatenate([array[:, unit:], array[:, :unit]], axis=1)


def first_unit(array):
    return lax.broadcasted_iota(jnp.int32, array.shape, 1) < array.shape[1] // 2


def quarters(*arrays):
    size = arrays[0].shape[0] // 4
    return jnp.concatenate(
        [array[at * size : (at + 1) * size] for at, array in enumerate(arrays)], axis=0
    )


def spectrum(forward, top, bottom):
    both = dot(forward[...], jnp.concatenate([top, bottom], axis=1))
    length, lanes = both.shape[0] // 2, top.shape[1]
    real, imag = both[:length, lanes:], both[length:, lanes:]
    plus, minus = (real + imag) * HALF_TURN, (real - imag) * HALF_TURN
    return (
        both[:length, :lanes] + quarters(minus, -plus, -minus, plus),
        both[length:, :lanes] + quarters(plus, minus, -plus, -minus),
    )


def inverse(backward, real, imag):
    length, lanes = real.shape
    plus, minus = real + imag, real - imag
    real = jnp.concatenate([real, quarters(plus, -minus, -plus, minus)], axis=1)
    imag = jnp.concatenate([imag, quarters(-minus, -plus, minus, plus)], axis=1)
    sums = dot(backward[...], jnp.concatenate([real, imag], axis=0).astype(BF16))
    return sums[:, :lanes] * (1.0 / length), sums[:, lanes:] * (HALF_TURN / length)


def times_conj(real, imag, other_real, other_imag):
    return real * other_real + imag * other_imag, imag * other_real - real * other_imag


def halves(array):
    size, lanes = array.shape[0] // 2, array.shape[1] // 2
    return [
        (array[part * size : (part + 1) * size, :lanes], array[part * size : (part + 1) * size, lanes:])
        for part in range(2)
    ]


def first_tick(gain, forward, backward, *rest):
    *chunks, out, spectra, held = rest
    gather_positions(chunks, first_steps(len(chunks)), held)
    parts = halves(held)
    real, imag = spectrum(forward, parts[0][0], parts[1][0])
    spectra[0], spectra[1] = real, imag
    convolved = inverse(backward, *times_conj(real, imag, swap(real), swap(imag)))
    gradients = []
    for part, (first, second) in enumerate(parts):
        kept = second.astype(F32)
        gradient = kept + swap(kept) * (convolved[part] + gain[...] * first.astype(F32))
        gradients.append(jnp.where(lax.axis_index("section") == 0, kept, gradient))
    top, bottom = gradients
    out[...] = jnp.where(first_unit(top), swap(top), bottom).astype(BF16)


def mixed_spectra(scale, forward, spectra, *rest):
    *chunks, post, weight, other, lag_spec, held = rest
    gather_positions(chunks, second_steps(len(chunks)), held)
    parts = halves(held)
    real, imag = spectrum(forward, parts[0][0], parts[1][0])
    low = first_unit(real)
    other[0] = jnp.where(low, spectra[0], real)
    other[1] = jnp.where(low, spectra[1], imag)
    lag_real, lag_imag = times_conj(spectra[0], spectra[1], swap(real), swap(imag))
    lag_spec[0] = jnp.where(low, 0.0, lag_real)
    lag_spec[1] = jnp.where(low, 0.0, lag_imag)
    for part, (_, gates) in enumerate(parts):
        gates = gates.astype(F32)
        low = first_unit(gates)
        post[part] = jnp.where(low, gates, swap(gates))
        weight[part] = jnp.where(low, swap(gates), scale)


def second_tick(gain, forward, backward, received, post, weight, other, lag_spec, *rest):
    *outs, stage = rest
    count, rows, _ = stage.shape
    carried = received[...].astype(F32)
    low = first_unit(carried)
    carried = [jnp.where(low, carried, swap(carried)), jnp.where(low, swap(carried), carried)]
    gated = [(post[part] * carried[part]).astype(BF16) for part in range(2)]
    real, imag = times_conj(*spectrum(forward, *gated), other[0], other[1])
    convolved = inverse(backward, real + lag_spec[0], imag + lag_spec[1])
    for part in range(2):
        skipped = jnp.where(low, gain[...] * gated[part].astype(F32), 0.0)
        result = weight[part] * (convolved[part] + skipped)
        result = jnp.where(low, carried[part] + result, result).astype(BF16)
        for block in range(count // 2):
            stage[part * (count // 2) + block] = result[block * rows : (block + 1) * rows]
    for step, out in zip([OWN, *last_steps(count)], outs):
        out[...] = stage[place(step)]


def unpack_gradient(*rest):
    *chunks, grad, stage = rest
    count = stage.shape[0]
    unit = stage.shape[2] // 2
    for step, chunk in zip([OWN, *last_steps(count)], chunks):
        stage[place(step)] = chunk[...]
    grad[0] = jnp.concatenate([stage[block][:, :unit] for block in range(count)], axis=1)


def unpack_lags(*rest):
    *refs, stage, lag_stage = rest
    count = stage.shape[0]
    chunks, lags = refs[:count], refs[count:]
    unit = stage.shape[2] // 2
    chan_index = lax.axis_index("chan")
    for step, chunk in zip([OWN, *last_steps(count)], chunks):
        stage[place(step)] = chunk[...]
    lag_grad = jnp.concatenate([stage[block][:, unit:] for block in range(count)], axis=1)
    lag_stage[...] = lag_grad.T
    for step, lag in enumerate(lags):
        width = lag.shape[0]
        lag[...] = lag_stage[pl.ds(pl.multiple_of((chan_index ^ step) * width, width), width), :]


def add_up(*refs):
    *lags, out = refs
    out[...] = functools.reduce(jnp.add, [lag[...].astype(F32) for lag in lags])


def exchange_chan(chunks):
    size = lax.axis_size("chan")
    return [chunks[0]] + [
        lax.ppermute(chunks[step], "chan", [(i, i ^ step) for i in range(size)])
        for step in reversed(range(1, size))
    ]


def exchange_seq(chunks, steps):
    size = lax.axis_size("seq")
    places = [(section, seq) for section in range(lax.axis_size("section")) for seq in range(size)]
    return [chunks[0]] + [
        lax.ppermute(
            chunk,
            ("section", "seq"),
            [
                (section * size + seq, section * size + (seq ^ step[section % 2]))
                for section, seq in places
            ],
        )
        for chunk, step in zip(chunks[1:], steps)
    ]


def body(forward, backward, *args):
    saved_input, pre_gate, post_gate, grad_held, loss_grad, filters, skip_gain = args
    seq_count = lax.axis_size("seq")
    chan_count = lax.axis_size("chan")
    section_count = lax.axis_size("section")
    _, tick_count, rows, width = saved_input.shape
    length = rows * seq_count
    unit = width // seq_count
    forward, backward = jnp.asarray(forward), jnp.asarray(backward)
    scale = 1.0 / math.sqrt(length * chan_count * tick_count)
    struct = jax.ShapeDtypeStruct
    chunk = struct((rows, 4 * unit), BF16)
    stage = struct((seq_count, rows, 4 * unit), BF16)
    held_rows = struct((length, 4 * unit), BF16)
    two_spectra = struct((2, length, 2 * unit), F32)
    two_parts = struct((2, length // 2, 2 * unit), F32)

    first = call(
        pack_first,
        [chunk] * seq_count,
        [stage, struct((4, rows, width), BF16), struct((rows, width), F32)],
        [pltpu.HBM] * 5,
        5,
    )(post_gate, grad_held, loss_grad, pre_gate, filters)
    *second, gain, forward, backward = call(
        pack_second,
        [chunk] * seq_count
        + [
            struct((1, 2 * unit), F32),
            struct(forward.shape, BF16),
            struct(backward.shape, BF16),
        ],
        [stage, struct((5, rows, width), BF16), struct((1, width), F32)],
        [pl.ANY] + [pltpu.HBM] * 6,
        8,
    )(first[0], saved_input, pre_gate, post_gate, skip_gain, forward, backward)
    first = exchange_seq(first, first_steps(seq_count))
    second = exchange_seq(second, second_steps(seq_count))

    gradient, spectra = call(
        first_tick,
        [struct((length // 2, 2 * unit), BF16), two_spectra],
        [held_rows],
    )(gain, forward, backward, *first)
    ring = [(i, (i - 1) % section_count) for i in range(section_count)]
    received = lax.ppermute(gradient, "section", ring)

    prepared = call(
        functools.partial(mixed_spectra, scale),
        [two_parts, two_parts, two_spectra, two_spectra],
        [held_rows],
    )(forward, spectra, *second)

    sorted_chunks = struct((seq_count, rows, 2 * unit), BF16)
    result = call(
        second_tick,
        [struct((rows, 2 * unit), BF16)] * seq_count,
        [sorted_chunks],
    )(gain, forward, backward, received, *prepared)
    result = exchange_seq(result, last_steps(seq_count))

    lag_width = width // chan_count
    lags = call(
        unpack_lags,
        [struct((lag_width, rows), BF16)] * chan_count,
        [sorted_chunks, struct((width, rows), BF16)],
    )(*result)
    lags = exchange_chan(lags)
    (grad_out,) = call(unpack_gradient, [struct((1, rows, width), BF16)], [sorted_chunks])(*result)
    (lag_grad,) = call(add_up, [struct((lag_width, rows), F32)])(*lags)
    return grad_out, lag_grad.T[None]


def solution(mesh):
    placed = (
        P("section", None, "seq", "chan"),
        P("section", None, "seq", "chan"),
        P("section", None, "seq", "chan"),
        P("section", "seq", "chan"),
        P("seq", "chan"),
        P("section", "seq", None),
        P("section", None),
    )

    def program(*args):
        return jax.shard_map(
            functools.partial(body, *transform_tables(args[0].shape[2])),
            mesh=mesh,
            in_specs=placed,
            out_specs=(P("section", "seq", "chan"), P("section", "seq", "chan")),
            check_vma=False,
        )(*args)

    return program
```
